32 devices in a mesh: dp: 4 (over x, core), fsdp: 8 (over z, y).
Axes of the slice: x: 2, y: 2, z: 4, core: 2. Of those that a mesh axis runs over, the one named last changes fastest.
Arguments:
- inputs: bfloat16 [2, 4, 512, 2048], P(None, 'dp', 'fsdp'), may hold values from -6 to 6
- cotangent: bfloat16 [2, 4, 512, 2048], P(None, 'dp', 'fsdp'), may hold values from -6 to 6
- norm_gain: bfloat16 [2048], P(('dp', 'fsdp')), may hold values from 0.5 to 1.5
- mixer_gain: bfloat16 [2048], P(('dp', 'fsdp')), may hold values from 0.5 to 1.5
- ffn_gain: bfloat16 [2048], P(('dp', 'fsdp')), may hold values from 0.5 to 1.5
- slack: bfloat16 [2048], P(('dp', 'fsdp')), may hold values from 2.99e-05 to 0.0601
- w_query: bfloat16 [2048, 2048], P(('dp', 'fsdp')), may hold values from -0.125 to 0.125
- w_forget: bfloat16 [2048, 2048], P(('dp', 'fsdp')), may hold values from -0.125 to 0.125
- w_input: bfloat16 [2048, 2048], P(('dp', 'fsdp')), may hold values from -0.125 to 0.125
- w_gate_out: bfloat16 [2048, 2048], P(('dp', 'fsdp')), may hold values from -0.125 to 0.125
- w_out: bfloat16 [2048, 2048], P(('dp', 'fsdp')), may hold values from -0.125 to 0.125
- w_gate: bfloat16 [2048, 5632], P(('dp', 'fsdp')), may hold values from -0.125 to 0.125
- w_up: bfloat16 [2048, 5632], P(('dp', 'fsdp')), may hold values from -0.125 to 0.125
- w_down: bfloat16 [5632, 2048], P(('dp', 'fsdp')), may hold values from -0.15625 to 0.15625
Outputs:
- output: float32 [2, 4, 512, 2048], P(None, 'dp', 'fsdp')
- input_grad: float32 [2, 4, 512, 2048], P(None, 'dp', 'fsdp')
- grad_norm_gain: float32 [2048], P(('dp', 'fsdp'))
- grad_mixer_gain: float32 [2048], P(('dp', 'fsdp'))
- grad_ffn_gain: float32 [2048], P(('dp', 'fsdp'))
- grad_slack: float32 [2048], P(('dp', 'fsdp'))
- grad_query: float32 [2048, 2048], P(('dp', 'fsdp'))
- grad_forget: float32 [2048, 2048], P(('dp', 'fsdp'))
- grad_input: float32 [2048, 2048], P(('dp', 'fsdp'))
- grad_gate_out: float32 [2048, 2048], P(('dp', 'fsdp'))
- grad_out: float32 [2048, 2048], P(('dp', 'fsdp'))
- grad_gate: float32 [2048, 5632], P(('dp', 'fsdp'))
- grad_up: float32 [2048, 5632], P(('dp', 'fsdp'))
- grad_down: float32 [5632, 2048], P(('dp', 'fsdp'))
The draws below stay inside these ranges and needn't reach their ends.
All inputs are finite; a program needn't handle non-finite values.
Results may differ from the reference program's by a relative error of at most 0.014.
Values may be sent and summed in bfloat16 or wider, within the bound.
No kernel may reach another device: no remote copies, remote signals or barrier semaphores. Data moves between devices by JAX's collectives and lax.ppermute only.
A program may use at most 512 MiB of HBM per device.

```python
import math
import jax
import jax.numpy as jnp
from jax import lax

D = 2048
HEADS = 16
HEAD = 128
FF = 5632
SPAN = 16
MICRO = 2
SEQS = 4
LENGTH = 512


def draw_slack(key, part):
    key = jax.random.fold_in(key, 7)
    bottom_log = math.log(0.0001)
    top_log = math.log(0.06)
    log_level = jax.random.uniform(key, (D,), jnp.float32, bottom_log, top_log)
    return jnp.exp(log_level).astype(jnp.bfloat16)


def block_levels(stream_key, dims, cuts, least, largest):
    def one(position, shards_of):
        steps = jax.random.uniform(jax.random.fold_in(jax.random.fold_in(stream_key, 6), position), (shards_of,), jnp.float32, least / len(cuts), largest / len(cuts))
        return jnp.repeat(jnp.exp(steps), dims[position] // shards_of).reshape((-1,) + (1,) * (len(dims) - position - 1))

    loudness = one(*cuts[0])
    for cut in cuts[1:]:
        loudness = loudness * one(*cut)
    return loudness


def scatter_about(rng, shape, width, most, cuts=(), held_as=jnp.bfloat16):
    values = jax.random.normal(rng, shape, jnp.float32) * width
    if len(cuts) > 0:
        values = block_levels(rng, shape, cuts, -0.22, 0.18) * values
    return jnp.clip(values, min=-most, max=most).astype(held_as)


def setup_inputs(seed: int = 0) -> dict:
    splits = jax.random.split(jax.random.key(seed), 15)
    return {
        "inputs": scatter_about(splits[0], (MICRO, SEQS, LENGTH, D), 1.0, 6.0, ((1, 4), (2, 8))),
        "cotangent": scatter_about(splits[1], (MICRO, SEQS, LENGTH, D), 1.0, 6.0, ((1, 4), (2, 8))),
        "norm_gain": jnp.clip(1.0 + 0.1 * jax.random.normal(splits[2], (D,), jnp.float32), 0.5, 1.5).astype(jnp.bfloat16),
        "mixer_gain": jnp.clip(1.0 + 0.1 * jax.random.normal(splits[3], (D,), jnp.float32), 0.5, 1.5).astype(jnp.bfloat16),
        "ffn_gain": jnp.clip(1.0 + 0.1 * jax.random.normal(splits[4], (D,), jnp.float32), 0.5, 1.5).astype(jnp.bfloat16),
        "slack": draw_slack(jax.random.fold_in(splits[14], 71), 0),
        "w_query": scatter_about(splits[6], (D, D), D ** -0.5, 0.125, ((0, 32),)),
        "w_forget": scatter_about(splits[7], (D, D), D ** -0.5, 0.125, ((0, 32),)),
        "w_input": scatter_about(splits[8], (D, D), D ** -0.5, 0.125, ((0, 32),)),
        "w_gate_out": scatter_about(splits[9], (D, D), D ** -0.5, 0.125, ((0, 32),)),
        "w_out": scatter_about(splits[10], (D, D), D ** -0.5, 0.125, ((0, 32),)),
        "w_gate": scatter_about(splits[11], (D, FF), D ** -0.5, 0.125, ((0, 32),)),
        "w_up": scatter_about(splits[12], (D, FF), D ** -0.5, 0.125, ((0, 32),)),
        "w_down": scatter_about(splits[13], (FF, D), (FF // 4) ** -0.5, 0.15625, ((0, 32),)),
    }


@jax.custom_vjp
def low(v):
    return lax.optimization_barrier(v.astype(jnp.bfloat16)).astype(jnp.float32)

@jax.custom_vjp
def low_back(v):
    return v

def low_keep(v):
    return (low(v), None)

def low_pass(kept, grad):
    return (grad,)

def back_keep(v):
    return (v, None)

def back_low(kept, grad):
    return (low(grad),)
low.defvjp(low_keep, low_pass)
low_back.defvjp(back_keep, back_low)

def precise_einsum(form, *operands):
    return jnp.einsum(form, *operands, precision=lax.Precision.HIGHEST)

def rms_scale(values, gain):
    return values * lax.rsqrt(lax.optimization_barrier(jnp.mean(values * values, axis=-1, keepdims=True)) + 1e-06) * gain

def forget_terms(forget_proj, slack):
    incoming_keys = slack * (1.0 - jax.nn.sigmoid(forget_proj))
    return (incoming_keys, jnp.log1p(-incoming_keys))

def gated_group_norm(mixed_out, gate_out, mixer_gain):
    gated = mixed_out * jax.nn.silu(gate_out)
    head_shape = gated.shape[:-1] + (HEADS, HEAD)
    grouped = gated.reshape(head_shape)
    centred = grouped - lax.optimization_barrier(jnp.mean(grouped, axis=-1, keepdims=True))
    scaled = centred * lax.rsqrt(lax.optimization_barrier(jnp.mean(centred * centred, axis=-1, keepdims=True)) + 1e-05)
    return scaled.reshape(gated.shape) * mixer_gain

def span_step(recurrent_state, pieces):
    query_rows, log_decay, incoming_keys, incoming_values = pieces
    cumulative_log = jnp.cumsum(log_decay, axis=1)
    positions = jnp.arange(query_rows.shape[1])
    causal = (positions[:, None] >= positions[None, :])[None, :, :, None, None]
    log_gap = cumulative_log[:, :, None] - cumulative_log[:, None, :]
    weight = jnp.where(causal, jnp.exp(jnp.where(causal, log_gap, 0.0)), 0.0)
    scores = precise_einsum('bthk,bshk,btshk->btsh', query_rows, incoming_keys, weight)
    inner_part = precise_einsum('btsh,bshv->bthv', scores, incoming_values)
    cross_block_part = precise_einsum('bthk,bhkv->bthv', query_rows * jnp.exp(cumulative_log), recurrent_state)
    closing_log_decay = cumulative_log[:, -1:]
    fresh_state = precise_einsum('bshk,bshv->bhkv', incoming_keys * jnp.exp(closing_log_decay - cumulative_log), incoming_values)
    recurrent_state = jnp.exp(closing_log_decay[:, 0])[..., None] * recurrent_state + fresh_state
    return (recurrent_state, inner_part + cross_block_part)

def recurrence(query_rows, log_decay, incoming_keys, incoming_values):
    batch_size, length = (query_rows.shape[0], query_rows.shape[1])
    blocks = length // SPAN

    def to_blocks(array):
        return jnp.moveaxis(array.reshape(batch_size, blocks, SPAN, HEADS, HEAD), 1, 0)
    start_state = jnp.zeros((batch_size, HEADS, HEAD, HEAD), jnp.float32)
    _, outputs = lax.scan(jax.checkpoint(span_step), start_state, (to_blocks(query_rows), to_blocks(log_decay), to_blocks(incoming_keys), to_blocks(incoming_values)))
    return jnp.moveaxis(outputs, 0, 1).reshape(batch_size, length, HEADS * HEAD)

def layer(tokens, params):
    norm_gain, mixer_gain, ffn_gain, slack, w_query, w_forget, w_input, w_gate_out, w_out, w_gate, w_up, w_down = params
    normed = low(rms_scale(tokens, norm_gain))
    query_rows = low_back(precise_einsum('btd,de->bte', normed, w_query))
    forget_proj = low_back(precise_einsum('btd,de->bte', normed, w_forget))
    incoming_values = low_back(precise_einsum('btd,de->bte', normed, w_input))
    gate_out = low_back(precise_einsum('btd,de->bte', normed, w_gate_out))
    incoming_keys, log_decay = forget_terms(forget_proj, slack)
    head_shape = tokens.shape[:-1] + (HEADS, HEAD)
    mixed_out = recurrence(query_rows.reshape(head_shape), log_decay.reshape(head_shape), incoming_keys.reshape(head_shape), incoming_values.reshape(head_shape))
    unit_normed = low(gated_group_norm(mixed_out, gate_out, mixer_gain))
    branch = low_back(precise_einsum('btd,de->bte', unit_normed, w_out))
    hidden = tokens + branch
    hidden_normed = low(rms_scale(hidden, ffn_gain))
    gate_proj = low_back(precise_einsum('btd,df->btf', hidden_normed, w_gate))
    up_proj = low_back(precise_einsum('btd,df->btf', hidden_normed, w_up))
    inner_part = low(jax.nn.silu(gate_proj) * up_proj)
    down_proj = low_back(precise_einsum('btf,fd->btd', inner_part, w_down))
    return hidden + down_proj

def reference(inputs, cotangent, norm_gain, mixer_gain, ffn_gain, slack, w_query, w_forget, w_input, w_gate_out, w_out, w_gate, w_up, w_down):
    params = tuple((weight.astype(jnp.float32) for weight in (norm_gain, mixer_gain, ffn_gain, slack, w_query, w_forget, w_input, w_gate_out, w_out, w_gate, w_up, w_down)))
    results, input_grads = ([], [])
    grad_sum = tuple((jnp.zeros_like(weight) for weight in params))
    for micro_index in range(MICRO):
        tokens = inputs[micro_index].astype(jnp.float32)
        result, pullback = jax.vjp(layer, tokens, params)
        d_tokens, d_params = pullback(cotangent[micro_index].astype(jnp.float32))
        results.append(result)
        input_grads.append(d_tokens)
        grad_sum = tuple((total + term for total, term in zip(grad_sum, d_params)))
    return (jnp.stack(results), jnp.stack(input_grads), grad_sum[0], grad_sum[1], grad_sum[2], grad_sum[3], grad_sum[4], grad_sum[5], grad_sum[6], grad_sum[7], grad_sum[8], grad_sum[9], grad_sum[10], grad_sum[11])
```

```python
import functools

import jax
import jax.numpy as jnp
from jax import lax
from jax.experimental import pallas as pl
from jax.experimental.pallas import tpu as pltpu
from jax.sharding import PartitionSpec as P

HEAD = 128
LANES = 128
HIGHEST = lax.Precision.HIGHEST
NN = (((1,), (0,)), ((), ()))
NT = (((1,), (1,)), ((), ()))
TN = (((0,), (0,)), ((), ()))


def ranks():
    return lax.axis_size("fsdp") // 2


def rank():
    return lax.axis_index("fsdp") // 2


def side():
    return lax.axis_index("fsdp") % 2


def pick(array, index, axis=0):
    return lax.dynamic_index_in_dim(array, index, axis, False)


def swapped(array):
    count = lax.axis_size("fsdp")
    return lax.ppermute(array, "fsdp", [(i, i ^ 1) for i in range(count)])


def turned(array, turn):
    count = lax.axis_size("fsdp")
    return lax.ppermute(array, "fsdp", [(i, (i + 2 * turn) % count) for i in range(count)])


def across(array, bit):
    count = lax.axis_size("dp")
    return lax.ppermute(array, "dp", [(i, i ^ bit) for i in range(count)])


def placed(pieces):
    whole = jnp.zeros((len(pieces),) + pieces[0][1].shape, pieces[0][1].dtype)
    for index, piece in pieces:
        whole = lax.dynamic_update_index_in_dim(whole, piece, index, 0)
    return whole


def to_side(*arrays):
    here = side()
    got = swapped(jnp.concatenate([pick(array, 1 - here) for array in arrays], axis=0))
    both = [placed([(here, pick(a, here)[0]), (1 - here, piece)]) for a, piece in zip(arrays, got)]
    return [rows.reshape((-1,) + rows.shape[2:]) for rows in both]


def from_side(rows):
    here = side()
    halves = rows.reshape((2, 1, rows.shape[0] // 2) + rows.shape[1:])
    got = swapped(pick(halves, 1 - here))
    return placed([(here, pick(halves, here)), (1 - here, got)])


def shifted(array, step, among=None):
    count = ranks()
    starts = [r for r in (range(count) if among is None else among) if 0 <= r + step < count]
    moves = [(2 * r + s, 2 * (r + step) + s) for r in starts for s in range(2)]
    return lax.ppermute(array, "fsdp", moves)


def ends_traded(array):
    last = lax.axis_size("fsdp") - 2
    moves = [(s, last + s) for s in range(2)] + [(last + s, s) for s in range(2)]
    return lax.ppermute(array, "fsdp", moves)


def gather_first(own):
    if ranks() != 4:
        return [turned(own, turn) for turn in range(1, ranks())]
    return [shifted(own, 1), shifted(own, -1), ends_traded(own)]


def gather_second(first):
    return [] if ranks() != 4 else [shifted(first[0], 1, (1, 2)), shifted(first[1], -1, (1, 2))]


def gathered(own, first, second):
    here = rank()
    if ranks() != 4:
        return jnp.concatenate([own] + first, axis=0)
    up, down, ends = first
    up2, down2 = second
    near = [jnp.where(here == 0, ends, up), jnp.where(here >= 2, up2, down2)]
    return jnp.concatenate([own] + near + [jnp.where(here == 3, ends, down)], axis=0)


def away_rows(operand):
    return operand[operand.shape[0] // ranks() :]


def own_rows(operand):
    return operand[: operand.shape[0] // ranks()]


def by_turn(away):
    return jnp.split(away.astype(jnp.bfloat16), ranks() - 1, axis=0)


def scatter_first(terms):
    if ranks() != 4:
        return [turned(term, -turn - 1) for turn, term in enumerate(terms)]
    ends = jnp.where(rank() == 0, terms[0], terms[2])
    return [shifted(terms[1], 1, (0, 1)), shifted(terms[1], -1, (2, 3)), ends_traded(ends)]


def scatter_second(terms, first):
    if ranks() != 4:
        return []
    up = terms[2].astype(jnp.float32) + first[0].astype(jnp.float32)
    down = terms[0].astype(jnp.float32) + first[1].astype(jnp.float32)
    return [shifted(up.astype(jnp.bfloat16), 1), shifted(down.astype(jnp.bfloat16), -1)]


def scattered(own, first, second):
    for piece in first if ranks() != 4 else first[2:] + second:
        own = own + piece.astype(jnp.float32)
    return own


def sync(*arrays):
    return lax.optimization_barrier(arrays)


def dp_bits():
    bits, bit = [], 1
    while bit < lax.axis_size("dp"):
        bits.append(bit)
        bit *= 2
    return bits


def routes(side_first):
    bits = [((bit, 0), functools.partial(across, bit=bit)) for bit in reversed(dp_bits())]
    return [((0, 1), swapped)] + bits if side_first else bits[:-1] + [((0, 1), swapped)] + bits[-1:]


def user_moves():
    dp, fsdp = lax.axis_size("dp"), lax.axis_size("fsdp")
    moves = []
    for block in range(dp * fsdp):
        user, part = divmod(block, 2 * dp)
        moves.append((block, (part // 2) * fsdp + 2 * user + part % 2))
    return moves


def to_users(rows):
    return lax.ppermute(rows, ("dp", "fsdp"), user_moves())


def to_owners(rows):
    return lax.ppermute(rows, ("dp", "fsdp"), [(b, a) for a, b in user_moves()])


def cut_kernel(order_ref, *refs):
    count = order_ref.shape[0]
    weights, pieces = refs[:-count], refs[-count:]
    for turn in range(count):
        start = 0
        for weight in weights:
            width = weight.shape[1] // (1 if weight.shape[1] == LANES else count)
            column = 0
            if weight.shape[1] != LANES:
                column = pl.multiple_of(order_ref[turn] * width, LANES)
            pieces[turn][:, start : start + width] = weight[:, pl.ds(column, width)]
            start += width


def cut_columns(order, *weights):
    count = ranks()
    rows = weights[0].shape[0]
    vmem = pl.BlockSpec(memory_space=pltpu.VMEM)
    width = sum(LANES if w.shape[1] == LANES else w.shape[1] // count for w in weights)
    return pl.pallas_call(
        cut_kernel,
        in_specs=[pl.BlockSpec(memory_space=pltpu.SMEM)] + [vmem] * len(weights),
        out_specs=[vmem] * count,
        out_shape=[jax.ShapeDtypeStruct((rows, width), weights[0].dtype)] * count,
        compiler_params=pltpu.CompilerParams(vmem_limit_bytes=24 * 1024 * 1024),
        name="cut_columns",
    )(order, *weights)


def join_kernel(order_ref, *refs):
    count = order_ref.shape[0]
    parts = (len(refs) - count - 1) // 2
    pieces, weights = refs[:count], refs[count : count + parts]
    grads, product = refs[count + parts : -1], refs[-1]
    total = jnp.zeros(product.shape, jnp.float32)
    for turn in range(count):
        start = 0
        for weight, grad in zip(weights, grads):
            width = weight.shape[1] // count
            columns = pl.ds(pl.multiple_of(order_ref[turn] * width, LANES), width)
            piece = pieces[turn][:, start : start + width].astype(jnp.float32)
            grad[:, columns] = piece
            term = piece * weight[:, columns].astype(jnp.float32)
            total = total + jnp.sum(term, axis=1, keepdims=True)
            start += width
    product[...] = total


def join_columns(order, pieces, weights):
    rows = weights[0].shape[0]
    vmem = pl.BlockSpec(memory_space=pltpu.VMEM)
    *grads, product = pl.pallas_call(
        join_kernel,
        in_specs=[pl.BlockSpec(memory_space=pltpu.SMEM)] + [vmem] * (len(pieces) + len(weights)),
        out_specs=[vmem] * (len(weights) + 1),
        out_shape=[jax.ShapeDtypeStruct(w.shape, jnp.float32) for w in weights]
        + [jax.ShapeDtypeStruct((rows, 1), jnp.float32)],
        compiler_params=pltpu.CompilerParams(vmem_limit_bytes=32 * 1024 * 1024),
        name="join_columns",
    )(order, *pieces, *weights)
    return grads, product[:, 0]


def assemble_kernel(place_ref, near_ref, far_ref, near_core_ref, far_core_ref, whole_ref, sems, *, marks):
    count = near_ref.shape[1]
    dp_index, here, first_rank = place_ref[0], place_ref[1], place_ref[2]
    copies = []
    for blocks, refs in ((0, (near_ref, far_ref)), (1, (near_core_ref, far_core_ref))):
        for outer in range(2):
            for inner in range(2):
                dp_mark, side_mark = marks[outer][inner]
                spot = jnp.bitwise_xor(dp_index, dp_mark + blocks)
                its_side = jnp.bitwise_xor(here, side_mark)
                for turn in range(count):
                    its_rank = lax.rem(first_rank - turn + count, count)
                    copies.append(
                        pltpu.make_async_copy(
                            refs[outer].at[inner, turn],
                            whole_ref.at[spot, its_rank, its_side],
                            sems.at[len(copies)],
                        )
                    )
                    copies[-1].start()
    for copy in copies:
        copy.wait()


def assembled(near, far, near_core, far_core, side_first):
    dp, (_, count, rows, columns) = lax.axis_size("dp"), near.shape
    big = dp // 2
    marks = (((0, 0), (0, 1)), ((big, 0), (big, 1))) if side_first else (((0, 0), (big, 0)), ((0, 1), (big, 1)))
    place = jnp.stack([lax.axis_index("dp"), side(), rank()]).astype(jnp.int32)
    anywhere = pl.BlockSpec(memory_space=pl.ANY)
    whole = pl.pallas_call(
        functools.partial(assemble_kernel, marks=marks),
        in_specs=[pl.BlockSpec(memory_space=pltpu.SMEM)] + [anywhere] * 4,
        out_specs=pl.BlockSpec(memory_space=pltpu.VMEM),
        out_shape=jax.ShapeDtypeStruct((dp, count, 2, rows, columns), near.dtype),
        scratch_shapes=[pltpu.SemaphoreType.DMA((8 * count,))],
        compiler_params=pltpu.CompilerParams(vmem_limit_bytes=24 * 1024 * 1024),
        cost_estimate=pl.CostEstimate(
            flops=0, bytes_accessed=32 * near.size, transcendentals=0
        ),
        name="assemble_rows",
    )(place, near, far, near_core, far_core)
    return whole.reshape(-1, columns)


def traded(pieces):
    return [pieces[0]] + [turned(piece, turn) for turn, piece in enumerate(pieces) if turn]


def turns(step):
    return (rank() + step * jnp.arange(ranks(), dtype=jnp.int32) + ranks()) % ranks()


def term_blocks(term):
    dp, count = lax.axis_size("dp"), ranks()
    bits = len(dp_bits())
    term = term.reshape((2,) * bits + (count, 2, term.shape[0] // (2 * dp * count), term.shape[-1]))
    return jnp.moveaxis(term, bits + 1, bits)


def shrunk(state, route):
    terms, marks = state
    mark, exchange = route
    axis = marks.index(mark)
    own = (lax.axis_index("dp") // mark[0]) % 2 if mark[0] else side()
    got = exchange(pick(terms, 1 - own, axis))
    total = pick(terms, own, axis).astype(jnp.float32) + got.astype(jnp.float32)
    return (total.astype(jnp.bfloat16), marks[:axis] + marks[axis + 1 :])


def block_marks():
    return [(bit, 0) for bit in reversed(dp_bits())] + [(0, 1)]


def peers():
    dp, fsdp = lax.axis_size("dp"), lax.axis_size("fsdp")
    return [[d * fsdp + 2 * r + s for d in range(dp) for s in range(2)] for r in range(fsdp // 2)]


def peers_gather(rows):
    return lax.all_gather(rows, ("dp", "fsdp"), tiled=True, axis_index_groups=peers())


def peers_scatter(terms):
    return lax.psum_scatter(
        terms, ("dp", "fsdp"), scatter_dimension=0, tiled=True, axis_index_groups=peers()
    )


def matmul(left_side, right_side):
    return jnp.dot(left_side, right_side, preferred_element_type=jnp.float32)


def outer_sum(left_side, right_side):
    return lax.dot_general(left_side, right_side, TN, preferred_element_type=jnp.float32)


def back_product(left_side, right_side):
    return lax.dot_general(left_side, right_side, NT, preferred_element_type=jnp.float32)


def dot(left, right, dims, precision=HIGHEST):
    return lax.dot_general(
        left, right, dims, precision=precision, preferred_element_type=jnp.float32
    )


def decayed(forget_proj, slack, lower):
    sig = jax.nn.sigmoid(forget_proj)
    keys = slack * (1.0 - sig)
    running = dot(lower, jnp.log1p(-keys), NN)
    return (sig, keys, running)


def triangle(size):
    rows = lax.broadcasted_iota(jnp.int32, (size, size), 0)
    columns = lax.broadcasted_iota(jnp.int32, (size, size), 1)
    return jnp.where(rows >= columns, 1.0, 0.0)


def normed_head(mixed, gate):
    sig = jax.nn.sigmoid(gate)
    silu = gate * sig
    gated = mixed * silu
    centred = gated - jnp.mean(gated, axis=-1, keepdims=True)
    inv = lax.rsqrt(jnp.mean(centred * centred, axis=-1, keepdims=True) + 1e-05)
    return (sig, silu, inv, centred * inv)


def forward_kernel(
    order_ref, query_ref, value_ref, slack_ref, gain_ref, unit_ref, mixed_ref, states_ref, state
):
    span = query_ref.shape[1]
    share = slack_ref.shape[1]

    @pl.when(pl.program_id(0) == 0)
    def _():
        state[...] = jnp.zeros_like(state)

    states_ref[0] = state[...]
    lower = triangle(span)
    _, keys, running = decayed(query_ref[0, :, share:], slack_ref[...], lower)
    grown = jnp.exp(running)
    queries = query_ref[0, :, :share] * grown
    keys = keys * jnp.exp(-running)
    for head in range(share // HEAD):
        here = slice(head * HEAD, (head + 1) * HEAD)
        gate_here = slice(share + head * HEAD, share + (head + 1) * HEAD)
        values = value_ref[0, :, here]
        before = state[head]
        scores = dot(queries[:, here], keys[:, here], NT) * lower
        mixed = dot(scores, values, NN) + dot(queries[:, here], before, NT)
        state[head] = (before + dot(values, keys[:, here], TN)) * grown[span - 1 :, here]
        mixed_ref[0, :, here] = mixed
        normed = normed_head(mixed, value_ref[0, :, gate_here])[3]
        unit_ref[0, :, here] = (normed * gain_ref[:, here]).astype(jnp.bfloat16)


def backward_kernel(
    order_ref,
    query_ref,
    value_ref,
    slack_ref,
    gain_ref,
    mixed_ref,
    states_ref,
    d_unit_ref,
    d_query_ref,
    d_value_ref,
    term_ref,
    back,
    carry,
):
    span = query_ref.shape[1]
    share = slack_ref.shape[1]

    @pl.when(pl.program_id(0) == 0)
    def _():
        back[...] = jnp.zeros_like(back)
        carry[...] = jnp.zeros_like(carry)
        term_ref[...] = jnp.zeros_like(term_ref)

    lower = triangle(span)
    slack = slack_ref[...]
    sig, raw_keys, running = decayed(query_ref[0, :, share:], slack, lower)
    grown, shrunk = jnp.exp(running), jnp.exp(-running)
    all_queries = query_ref[0, :, :share] * grown
    all_keys = raw_keys * shrunk
    d_running, d_raw_keys = [], []
    for head in range(share // HEAD):
        here = slice(head * HEAD, (head + 1) * HEAD)
        there = slice(share + head * HEAD, share + (head + 1) * HEAD)
        queries, keys = all_queries[:, here], all_keys[:, here]
        values, gate = value_ref[0, :, here], value_ref[0, :, there]
        mixed = mixed_ref[0, :, here]
        d_unit = d_unit_ref[0, :, here]
        sig_gate, silu, inv, normed = normed_head(mixed, gate)
        term_ref[1:2, here] += jnp.sum(d_unit * normed, axis=0, keepdims=True)
        d_n = d_unit * gain_ref[:, here]
        d_gated = inv * (
            d_n
            - jnp.mean(d_n, axis=-1, keepdims=True)
            - normed * jnp.mean(d_n * normed, axis=-1, keepdims=True)
        )
        d_mixed = d_gated * silu
        d_gate = d_gated * mixed * sig_gate * (1.0 + gate * (1.0 - sig_gate))
        d_value_ref[0, :, there] = d_gate.astype(jnp.bfloat16)
        before = states_ref[0, head]
        after_grad = back[head] * grown[span - 1 :, here]
        scores = dot(queries, keys, NT) * lower
        d_scores = dot(d_mixed, values, NT) * lower
        d_queries = dot(d_scores, keys, NN) + dot(d_mixed, before, NN)
        d_keys = dot(d_scores, queries, TN) + dot(values, after_grad, NN)
        d_values = dot(scores, d_mixed, TN) + dot(keys, after_grad, NT)
        before_grad = dot(d_mixed, queries, TN) + after_grad
        d_value_ref[0, :, here] = d_values.astype(jnp.bfloat16)
        d_query_ref[0, :, here] = (d_queries * grown[:, here]).astype(jnp.bfloat16)
        back[head] = before_grad
        d_running.append(queries * d_queries - keys * d_keys)
        d_raw_keys.append(d_keys * shrunk[:, here])
    d_log = dot(lower, jnp.concatenate(d_running, axis=-1), TN) + carry[...]
    for head in range(share // HEAD):
        here = slice(head * HEAD, (head + 1) * HEAD)
        carry[:, here] = jnp.sum(states_ref[0, head] * back[head], axis=0, keepdims=True)
    e = jnp.concatenate(d_raw_keys, axis=-1) - d_log / (1.0 - raw_keys)
    term_ref[0:1, :] += jnp.sum(e * (1.0 - sig), axis=0, keepdims=True)
    d_query_ref[0, :, share:] = (-e * slack * sig * (1.0 - sig)).astype(jnp.bfloat16)


def row_block(step, order_ref):
    return (order_ref[step], 0, 0)


def state_block(step, order_ref):
    return (order_ref[step], 0, 0, 0)


def fixed_block(step, order_ref):
    return (0, 0)


def run_forward(order, queries, values, slack, gain):
    blocks, span, columns = queries.shape
    share = columns // 2
    heads = share // HEAD
    return pl.pallas_call(
        forward_kernel,
        grid_spec=pltpu.PrefetchScalarGridSpec(
            num_scalar_prefetch=1,
            grid=(blocks,),
            in_specs=[
                pl.BlockSpec((1, span, columns), row_block),
                pl.BlockSpec((1, span, columns), row_block),
                pl.BlockSpec((1, share), fixed_block),
                pl.BlockSpec((1, share), fixed_block),
            ],
            out_specs=[
                pl.BlockSpec((1, span, share), row_block),
                pl.BlockSpec((1, span, share), row_block),
                pl.BlockSpec((1, heads, HEAD, HEAD), state_block),
            ],
            scratch_shapes=[pltpu.VMEM((heads, HEAD, HEAD), jnp.float32)],
        ),
        out_shape=[
            jax.ShapeDtypeStruct((blocks, span, share), jnp.bfloat16),
            jax.ShapeDtypeStruct((blocks, span, share), jnp.float32),
            jax.ShapeDtypeStruct((blocks, heads, HEAD, HEAD), jnp.float32),
        ],
        compiler_params=pltpu.CompilerParams(vmem_limit_bytes=24 * 1024 * 1024),
        cost_estimate=pl.CostEstimate(
            flops=40 * queries.size * span, bytes_accessed=20 * queries.size, transcendentals=2 * queries.size
        ),
        name="recurrence_forward",
    )(order, queries, values, slack, gain)


def run_backward(order, queries, values, slack, gain, mixed, states, d_unit):
    blocks, span, columns = queries.shape
    share = columns // 2
    heads = share // HEAD
    return pl.pallas_call(
        backward_kernel,
        grid_spec=pltpu.PrefetchScalarGridSpec(
            num_scalar_prefetch=1,
            grid=(blocks,),
            in_specs=[
                pl.BlockSpec((1, span, columns), row_block),
                pl.BlockSpec((1, span, columns), row_block),
                pl.BlockSpec((1, share), fixed_block),
                pl.BlockSpec((1, share), fixed_block),
                pl.BlockSpec((1, span, share), row_block),
                pl.BlockSpec((1, heads, HEAD, HEAD), state_block),
                pl.BlockSpec((1, span, share), row_block),
            ],
            out_specs=[
                pl.BlockSpec((1, span, columns), row_block),
                pl.BlockSpec((1, span, columns), row_block),
                pl.BlockSpec((2, share), fixed_block),
            ],
            scratch_shapes=[
                pltpu.VMEM((heads, HEAD, HEAD), jnp.float32),
                pltpu.VMEM((1, share), jnp.float32),
            ],
        ),
        out_shape=[
            jax.ShapeDtypeStruct((blocks, span, columns), jnp.bfloat16),
            jax.ShapeDtypeStruct((blocks, span, columns), jnp.bfloat16),
            jax.ShapeDtypeStruct((2, share), jnp.float32),
        ],
        compiler_params=pltpu.CompilerParams(vmem_limit_bytes=32 * 1024 * 1024),
        cost_estimate=pl.CostEstimate(
            flops=80 * queries.size * span, bytes_accessed=30 * queries.size, transcendentals=2 * queries.size
        ),
        name="recurrence_backward",
    )(order, queries, values, slack, gain, mixed, states, d_unit)


def inverse_rms(values):
    return lax.rsqrt(jnp.mean(values * values, axis=-1, keepdims=True) + 1e-06)


def unscaled_grad(d_scaled, scaled, inverse):
    return inverse * (d_scaled - scaled * jnp.mean(d_scaled * scaled, axis=-1, keepdims=True))


def on_device(
    inputs,
    cotangent,
    norm_gain,
    mixer_gain,
    ffn_gain,
    slack,
    w_query,
    w_forget,
    w_input,
    w_gate_out,
    w_out,
    w_gate,
    w_up,
    w_down,
):
    width = inputs.shape[-1]
    dp, count, here = lax.axis_size("dp"), ranks(), rank()
    float32, bfloat16 = jnp.float32, jnp.bfloat16
    sending, taking = turns(1), turns(-1)
    mixer_weights = (w_query, w_forget, w_input, w_gate_out)
    ffn_weights = (w_gate, w_up)
    core, big = 1, dp // 2

    gains = jnp.stack([norm_gain, ffn_gain, mixer_gain, slack], axis=1)
    gains = jnp.pad(gains, ((0, 0), (0, LANES - gains.shape[1])))
    cut = traded(cut_columns(sending, w_query, w_forget, gains, w_input, w_gate_out))
    users_out = to_users(w_out)
    own_in, own_d = to_side(inputs, cotangent)
    own_in, own_d, cut = sync(own_in, own_d, cut)

    first_in = gather_first(own_in)
    split = 2 * (width // count) + LANES
    query_cut = jnp.stack([piece[:, :split] for piece in cut])
    value_cut = jnp.stack([piece[:, split:] for piece in cut])
    query_near = jnp.stack([query_cut, across(query_cut, big)])
    value_near = jnp.stack([value_cut, swapped(value_cut)])
    first_in, query_near, value_near, users_out = sync(first_in, query_near, value_near, users_out)

    second_in = gather_second(first_in)
    query_far = swapped(query_near)
    value_far = across(value_near, big)
    mixer_out = peers_gather(users_out)
    second_in, query_far, value_far, late_gate, late_up, late_down = sync(
        second_in, query_far, value_far, w_gate, w_up, w_down
    )

    query_blocks = (query_near, query_far, across(query_near, core), across(query_far, core))
    value_blocks = (value_near, value_far, across(value_near, core), across(value_far, core))
    raw_in = gathered(own_in, first_in, second_in)
    raw_in, query_blocks, value_blocks = sync(raw_in, query_blocks, value_blocks)

    cut = traded(cut_columns(sending, late_gate, late_up))
    query_in = assembled(*query_blocks, False)
    value_in = assembled(*value_blocks, True)
    share = value_in.shape[-1]
    gains = jnp.transpose(query_in[:, share:])[:4].astype(float32)
    gain_first, gain_second = gains[0], gains[1]
    here_gains = lax.dynamic_slice(gains, (2, here * (width // count)), (2, width // count))
    mixer_gain_here, slack_here = here_gains[:1], here_gains[1:]
    query_in = query_in[:, :share]

    all_tokens = raw_in.astype(float32)
    rows_in = (all_tokens * inverse_rms(all_tokens) * gain_first).astype(bfloat16)
    queries = matmul(rows_in, query_in).reshape(count, -1, share)
    values = matmul(rows_in, value_in).reshape(count, -1, share)
    unit, mixed, states = run_forward(taking, queries, values, slack_here, mixer_gain_here)
    rows_unit = unit.reshape(-1, unit.shape[-1])
    branch_terms = by_turn(matmul(away_rows(rows_unit), mixer_out))
    branch_terms, cut, late_down = sync(branch_terms, cut, late_down)

    branch_first = scatter_first(branch_terms)
    branch_own = matmul(own_rows(rows_unit), mixer_out)
    units = cut[0].shape[-1] // 2
    gate_cut = jnp.stack([piece[:, :units] for piece in cut])
    up_cut = jnp.stack([piece[:, units:] for piece in cut])
    gate_near = jnp.stack([gate_cut, across(gate_cut, big)])
    up_near = jnp.stack([up_cut, swapped(up_cut)])
    branch_first, branch_own, gate_near, up_near = sync(branch_first, branch_own, gate_near, up_near)

    branch_second = scatter_second(branch_terms, branch_first)
    gate_far = swapped(gate_near)
    up_far = across(up_near, big)
    users_down = to_users(late_down)
    tokens = own_in.astype(float32)
    hidden = tokens + scattered(branch_own, branch_first, branch_second)
    second_inverse = inverse_rms(hidden)
    hidden_hat = hidden * second_inverse
    own_mid = (hidden_hat * gain_second).astype(bfloat16)
    own_mid, users_down = sync(own_mid, users_down)

    first_mid = gather_first(own_mid)
    down = peers_gather(users_down)
    first_mid, gate_far, up_far = sync(first_mid, gate_far, up_far)

    second_mid = gather_second(first_mid)
    gate_blocks = (gate_near, gate_far, across(gate_near, core), across(gate_far, core))
    up_blocks = (up_near, up_far, across(up_near, core), across(up_far, core))
    second_mid, gate_blocks, up_blocks, late_d = sync(second_mid, gate_blocks, up_blocks, own_d)

    first_d = gather_first(late_d)
    rows_mid = gathered(own_mid, first_mid, second_mid)
    gate_in = assembled(*gate_blocks, False)
    gate_proj = matmul(rows_mid, gate_in)
    first_d, gate_proj = sync(first_d, gate_proj)

    second_d = gather_second(first_d)
    up_in = assembled(*up_blocks, True)
    up_proj = matmul(rows_mid, up_in)
    second_d, up_proj = sync(second_d, up_proj)

    rows_d = gathered(own_d, first_d, second_d)
    sig = jax.nn.sigmoid(gate_proj)
    inner = (gate_proj * sig * up_proj).astype(bfloat16)
    d_inner = back_product(rows_d, down)
    d_gate = (d_inner * up_proj * sig * (1.0 + gate_proj * (1.0 - sig))).astype(bfloat16)
    d_up = (d_inner * gate_proj * sig).astype(bfloat16)

    def hidden_product(cut):
        return back_product(cut(d_gate), gate_in) + back_product(cut(d_up), up_in)

    mid_terms = by_turn(hidden_product(away_rows))
    mid_terms, d_gate, d_up = sync(mid_terms, d_gate, d_up)

    mid_first = scatter_first(mid_terms)
    mid_own = hidden_product(own_rows)
    gate_term = term_blocks(outer_sum(rows_mid, d_gate).astype(bfloat16))
    mid_first, mid_own, gate_term = sync(mid_first, mid_own, gate_term)

    mid_second = scatter_second(mid_terms, mid_first)
    up_term = term_blocks(outer_sum(rows_mid, d_up).astype(bfloat16))
    d_hidden = own_d.astype(float32) + unscaled_grad(
        scattered(mid_own, mid_first, mid_second) * gain_second, hidden_hat, second_inverse
    )
    own_branch = d_hidden.astype(bfloat16)
    own_branch, up_term = sync(own_branch, up_term)

    first_branch = gather_first(own_branch)
    gate_state = shrunk((gate_term, block_marks()), ((core, 0), functools.partial(across, bit=core)))
    up_state = shrunk((up_term, block_marks()), ((core, 0), functools.partial(across, bit=core)))
    out_terms = by_turn(matmul(away_rows(inner), down))
    down_sum = peers_scatter(outer_sum(inner, rows_d).astype(bfloat16))
    first_branch, gate_total, up_total, out_terms = sync(
        first_branch, gate_state[0], up_state[0], out_terms
    )

    by_big, by_side = ((big, 0), functools.partial(across, bit=big)), ((0, 1), swapped)
    second_branch = gather_second(first_branch)
    gate_state = shrunk((gate_total, gate_state[1]), by_side)
    up_state = shrunk((up_total, up_state[1]), by_big)
    out_own = matmul(own_rows(inner), down)
    second_branch, out_own, gate_total, up_total = sync(
        second_branch, out_own, gate_state[0], up_state[0]
    )

    out_first = scatter_first(out_terms)
    gate_state = shrunk((gate_total, gate_state[1]), by_big)
    up_state = shrunk((up_total, up_state[1]), by_side)
    rows_branch = gathered(own_branch, first_branch, second_branch)
    d_unit = back_product(rows_branch, mixer_out).reshape(count, -1, mixer_out.shape[0])
    out_sum = peers_scatter(outer_sum(rows_unit, rows_branch).astype(bfloat16))
    d_queries, d_values, terms = run_backward(
        taking[::-1], queries, values, slack_here, mixer_gain_here, mixed, states, d_unit
    )
    d_queries = d_queries.reshape(-1, share)
    d_values = d_values.reshape(-1, share)

    def token_product(cut):
        return back_product(cut(d_queries), query_in) + back_product(cut(d_values), value_in)

    in_terms = by_turn(token_product(away_rows))
    in_terms, d_queries, d_values, out_first, gate_total, up_total = sync(
        in_terms, d_queries, d_values, out_first, gate_state[0], up_state[0]
    )

    in_first = scatter_first(in_terms)
    query_term = term_blocks(outer_sum(rows_in, d_queries).astype(bfloat16))
    value_term = term_blocks(outer_sum(rows_in, d_values).astype(bfloat16))
    by_core = ((core, 0), functools.partial(across, bit=core))
    query_state = shrunk((query_term, block_marks()), by_core)
    value_state = shrunk((value_term, block_marks()), by_core)
    in_own = token_product(own_rows)
    terms = jnp.transpose(terms.reshape(2, 2 * dp, -1), (1, 0, 2))
    terms = peers_scatter(terms.reshape(2 * dp, -1))
    in_first, in_own, query_total, value_total = sync(
        in_first, in_own, query_state[0], value_state[0]
    )

    in_second = scatter_second(in_terms, in_first)
    query_state = shrunk((query_total, query_state[1]), by_side)
    value_state = shrunk((value_total, value_state[1]), by_big)
    in_second, query_total, value_total = sync(in_second, query_state[0], value_state[0])

    out_second = scatter_second(out_terms, out_first)
    query_state = shrunk((query_total, query_state[1]), by_big)
    value_state = shrunk((value_total, value_state[1]), by_side)
    output = hidden + scattered(out_own, out_first, out_second)
    first_inverse = inverse_rms(tokens)
    d_normed = scattered(in_own, in_first, in_second)
    input_grad = d_hidden + unscaled_grad(
        d_normed * gain_first, tokens * first_inverse, first_inverse
    )
    query_total, value_total, output, input_grad = sync(
        query_state[0], value_state[0], output, input_grad
    )

    def parts(*totals):
        picked = [[pick(total, sending[turn]) for total in totals] for turn in range(count)]
        return traded([jnp.concatenate(pieces, axis=-1) for pieces in picked])

    ffn_parts = parts(gate_total, up_total)
    output, input_grad = from_side(output), from_side(input_grad)
    ffn_parts, late_terms, down_sum, out_sum, query_total, value_total = sync(
        ffn_parts, terms, down_sum, out_sum, query_total, value_total
    )

    mixer_parts = parts(query_total, value_total)
    out_rows = out_sum.shape[0]
    sums = to_owners(jnp.concatenate([out_sum, down_sum], axis=0))
    grad_out, grad_down = sums[:out_rows], sums[out_rows:]
    terms = to_owners(late_terms).reshape(2, -1)
    grads_ffn, ffn_product = join_columns(taking, ffn_parts, ffn_weights)
    grads_mixer, mixer_product = join_columns(taking, mixer_parts, mixer_weights)

    return (
        output,
        input_grad,
        mixer_product / norm_gain.astype(float32),
        terms[1],
        ffn_product / ffn_gain.astype(float32),
        terms[0],
        *grads_mixer,
        grad_out.astype(float32),
        *grads_ffn,
        grad_down.astype(float32),
    )


def solution(mesh):
    in_specs = (
        P(None, "dp", "fsdp", None),
        P(None, "dp", "fsdp", None),
        P(("dp", "fsdp")),
        P(("dp", "fsdp")),
        P(("dp", "fsdp")),
        P(("dp", "fsdp")),
        P(("dp", "fsdp"), None),
        P(("dp", "fsdp"), None),
        P(("dp", "fsdp"), None),
        P(("dp", "fsdp"), None),
        P(("dp", "fsdp"), None),
        P(("dp", "fsdp"), None),
        P(("dp", "fsdp"), None),
        P(("dp", "fsdp"), None),
    )
    out_specs = (
        P(None, "dp", "fsdp", None),
        P(None, "dp", "fsdp", None),
        P(("dp", "fsdp")),
        P(("dp", "fsdp")),
        P(("dp", "fsdp")),
        P(("dp", "fsdp")),
        P(("dp", "fsdp"), None),
        P(("dp", "fsdp"), None),
        P(("dp", "fsdp"), None),
        P(("dp", "fsdp"), None),
        P(("dp", "fsdp"), None),
        P(("dp", "fsdp"), None),
        P(("dp", "fsdp"), None),
        P(("dp", "fsdp"), None),
    )
    return jax.shard_map(
        on_device, mesh=mesh, in_specs=in_specs, out_specs=out_specs, check_vma=False
    )
```

```python
import functools

import jax
import jax.numpy as jnp
from jax import lax
from jax.experimental import pallas as pl
from jax.experimental.pallas import tpu as pltpu
from jax.sharding import PartitionSpec as P

HEAD = 128
LANES = 128
VMEM_BYTES = 56 * 1024 * 1024
HIGHEST = lax.Precision.HIGHEST
NN = (((1,), (0,)), ((), ()))
NT = (((1,), (1,)), ((), ()))
TN = (((0,), (0,)), ((), ()))


def ranks():
    return lax.axis_size("fsdp") // 2


def rank():
    return lax.axis_index("fsdp") // 2


def side():
    return lax.axis_index("fsdp") % 2


def pick(array, index, axis=0):
    return lax.dynamic_index_in_dim(array, index, axis, False)


def swapped(array):
    count = lax.axis_size("fsdp")
    return lax.ppermute(array, "fsdp", [(i, i ^ 1) for i in range(count)])


def turned(array, turn):
    count = lax.axis_size("fsdp")
    return lax.ppermute(array, "fsdp", [(i, (i + 2 * turn) % count) for i in range(count)])


def across(array, bit):
    count = lax.axis_size("dp")
    return lax.ppermute(array, "dp", [(i, i ^ bit) for i in range(count)])


def placed(pieces):
    whole = jnp.zeros((len(pieces),) + pieces[0][1].shape, pieces[0][1].dtype)
    for index, piece in pieces:
        whole = lax.dynamic_update_index_in_dim(whole, piece, index, 0)
    return whole


def to_side(*arrays):
    here = side()
    got = swapped(jnp.concatenate([pick(array, 1 - here) for array in arrays], axis=0))
    both = [placed([(here, pick(a, here)[0]), (1 - here, piece)]) for a, piece in zip(arrays, got)]
    return [rows.reshape((-1,) + rows.shape[2:]) for rows in both]


def from_side(*arrays):
    here = side()
    halves = [rows.reshape((2, 1, rows.shape[0] // 2) + rows.shape[1:]) for rows in arrays]
    got = swapped(jnp.concatenate([pick(half, 1 - here) for half in halves], axis=0))
    return [
        placed([(here, pick(half, here)), (1 - here, piece[None])]) for half, piece in zip(halves, got)
    ]


def shifted(array, step, among=None):
    count = ranks()
    starts = [r for r in (range(count) if among is None else among) if 0 <= r + step < count]
    moves = [(2 * r + s, 2 * (r + step) + s) for r in starts for s in range(2)]
    return lax.ppermute(array, "fsdp", moves)


def ends_traded(array):
    last = lax.axis_size("fsdp") - 2
    moves = [(s, last + s) for s in range(2)] + [(last + s, s) for s in range(2)]
    return lax.ppermute(array, "fsdp", moves)


def gather_first(own, relay=True):
    if ranks() != 4 or not relay:
        return [turned(own, turn) for turn in range(1, ranks())]
    return [shifted(own, 1), shifted(own, -1), ends_traded(own)]


def gather_second(first):
    return [] if ranks() != 4 else [shifted(first[0], 1, (1, 2)), shifted(first[1], -1, (1, 2))]


def gathered_directly(own, pieces):
    return jnp.concatenate([own] + pieces, axis=0)


def gathered(own, first, second):
    here = rank()
    if ranks() != 4:
        return jnp.concatenate([own] + first, axis=0)
    up, down, ends = first
    up2, down2 = second
    near = [jnp.where(here == 0, ends, up), jnp.where(here >= 2, up2, down2)]
    return jnp.concatenate([own] + near + [jnp.where(here == 3, ends, down)], axis=0)


def away_rows(operand):
    return operand[operand.shape[0] // ranks() :]


def own_rows(operand):
    return operand[: operand.shape[0] // ranks()]


def by_turn(away):
    return jnp.split(away.astype(jnp.bfloat16), ranks() - 1, axis=0)


def scatter_first(terms):
    if ranks() != 4:
        return [turned(term, -turn - 1) for turn, term in enumerate(terms)]
    ends = jnp.where(rank() == 0, terms[0], terms[2])
    return [shifted(terms[1], 1, (0, 1)), shifted(terms[1], -1, (2, 3)), ends_traded(ends)]


def scatter_second(terms, first):
    if ranks() != 4:
        return []
    up = terms[2].astype(jnp.float32) + first[0].astype(jnp.float32)
    down = terms[0].astype(jnp.float32) + first[1].astype(jnp.float32)
    return [shifted(up.astype(jnp.bfloat16), 1), shifted(down.astype(jnp.bfloat16), -1)]


def scattered(own, first, second):
    for piece in first if ranks() != 4 else first[2:] + second:
        own = own + piece.astype(jnp.float32)
    return own


def sync(*arrays):
    return lax.optimization_barrier(arrays)


def dp_bits():
    bits, bit = [], 1
    while bit < lax.axis_size("dp"):
        bits.append(bit)
        bit *= 2
    return bits


def routes(side_first):
    bits = [((bit, 0), functools.partial(across, bit=bit)) for bit in reversed(dp_bits())]
    return [((0, 1), swapped)] + bits if side_first else bits[:-1] + [((0, 1), swapped)] + bits[-1:]


def user_moves():
    dp, fsdp = lax.axis_size("dp"), lax.axis_size("fsdp")
    moves = []
    for block in range(dp * fsdp):
        user, part = divmod(block, 2 * dp)
        moves.append((block, (part // 2) * fsdp + 2 * user + part % 2))
    return moves


def to_users(rows):
    return lax.ppermute(rows, ("dp", "fsdp"), user_moves())


def to_owners(rows):
    return lax.ppermute(rows, ("dp", "fsdp"), [(b, a) for a, b in user_moves()])


def for_rank(wanted, body, aligned):
    if aligned:
        body(wanted)
        return
    for number in range(ranks()):
        pl.when(wanted == number)(functools.partial(body, number))


def columns_of(number, chunk, weight, chunks, count):
    width = weight.shape[1] // (chunks * count)
    start = chunk * (weight.shape[1] // chunks) + number * width
    return pl.ds(start if isinstance(number, int) else pl.multiple_of(start, LANES), width)


def cut_kernel(order_ref, *refs, chunks):
    count = order_ref.shape[0]
    weights, pieces = refs[:-count], refs[-count:]
    for turn in range(count):

        def cut(number, turn=turn):
            start = 0
            for weight in weights:
                if weight.shape[1] == LANES:
                    pieces[turn][:, start : start + LANES] = weight[...]
                    start += LANES
                    continue
                for chunk in range(chunks):
                    columns = columns_of(number, chunk, weight, chunks, count)
                    pieces[turn][:, start : start + columns.size] = weight[:, columns]
                    start += columns.size

        widths = [w.shape[1] // (chunks * count) for w in weights if w.shape[1] != LANES]
        for_rank(order_ref[turn], cut, all(width % LANES == 0 for width in widths))


def cut_columns(order, weights, chunks):
    count = ranks()
    rows = weights[0].shape[0]
    vmem = pl.BlockSpec(memory_space=pltpu.VMEM)
    width = sum(LANES if w.shape[1] == LANES else w.shape[1] // count for w in weights)
    return pl.pallas_call(
        functools.partial(cut_kernel, chunks=chunks),
        in_specs=[pl.BlockSpec(memory_space=pltpu.SMEM)] + [vmem] * len(weights),
        out_specs=[vmem] * count,
        out_shape=[jax.ShapeDtypeStruct((rows, width), weights[0].dtype)] * count,
        compiler_params=pltpu.CompilerParams(vmem_limit_bytes=VMEM_BYTES),
        name="cut_columns",
    )(order, *weights)


def join_kernel(order_ref, *refs, chunks):
    count = order_ref.shape[0]
    parts = (len(refs) - count - 1) // 2
    pieces, weights = refs[:count], refs[count : count + parts]
    grads, product = refs[count + parts : -1], refs[-1]
    product[...] = jnp.zeros(product.shape, jnp.float32)
    for turn in range(count):

        def join(number, turn=turn):
            start = 0
            total = jnp.zeros(product.shape, jnp.float32)
            for weight, grad in zip(weights, grads):
                for chunk in range(chunks):
                    columns = columns_of(number, chunk, weight, chunks, count)
                    piece = pieces[turn][:, start : start + columns.size].astype(jnp.float32)
                    grad[:, columns] = piece
                    term = piece * weight[:, columns].astype(jnp.float32)
                    total = total + jnp.sum(term, axis=1, keepdims=True)
                    start += columns.size
            product[...] += total

        widths = [w.shape[1] // (chunks * count) for w in weights]
        for_rank(order_ref[turn], join, all(width % LANES == 0 for width in widths))


def join_columns(order, pieces, weights, chunks):
    rows = weights[0].shape[0]
    vmem = pl.BlockSpec(memory_space=pltpu.VMEM)
    *grads, product = pl.pallas_call(
        functools.partial(join_kernel, chunks=chunks),
        in_specs=[pl.BlockSpec(memory_space=pltpu.SMEM)] + [vmem] * (len(pieces) + len(weights)),
        out_specs=[vmem] * (len(weights) + 1),
        out_shape=[jax.ShapeDtypeStruct(w.shape, jnp.float32) for w in weights]
        + [jax.ShapeDtypeStruct((rows, 1), jnp.float32)],
        compiler_params=pltpu.CompilerParams(vmem_limit_bytes=VMEM_BYTES),
        cost_estimate=pl.CostEstimate(
            flops=0, bytes_accessed=40 * sum(w.size for w in weights), transcendentals=0
        ),
        name="join_columns",
    )(order, *pieces, *weights)
    return grads, product[:, 0]


def assemble_kernel(place_ref, *refs, marks):
    (*blocks, sems), wholes = refs[:4] + refs[-1:], refs[4:-1]
    count = blocks[0].shape[1]
    dp_index, here, first_rank = place_ref[0], place_ref[1], place_ref[2]
    copies = []
    for core in range(2):
        for outer in range(2):
            block = blocks[2 * core + outer]
            for inner in range(2):
                dp_mark, side_mark = marks[outer][inner]
                spot = jnp.bitwise_xor(dp_index, dp_mark + core)
                its_side = jnp.bitwise_xor(here, side_mark)
                for turn in range(count):
                    its_rank = lax.rem(first_rank - turn + count, count)
                    start = 0
                    for whole in wholes:
                        columns = whole.shape[-1]
                        source = block.at[inner, turn, :, pl.ds(start, columns)]
                        target = whole.at[spot, its_rank, its_side]
                        copies.append(pltpu.make_async_copy(source, target, sems.at[len(copies)]))
                        copies[-1].start()
                        start += columns
    for copy in copies:
        copy.wait()


def assembled(near, far, near_core, far_core, side_first, widths):
    dp, (_, count, rows, _) = lax.axis_size("dp"), near.shape
    big = dp // 2
    marks = (((0, 0), (0, 1)), ((big, 0), (big, 1))) if side_first else (((0, 0), (big, 0)), ((0, 1), (big, 1)))
    place = jnp.stack([lax.axis_index("dp"), side(), rank()]).astype(jnp.int32)
    anywhere = pl.BlockSpec(memory_space=pl.ANY)
    wholes = pl.pallas_call(
        functools.partial(assemble_kernel, marks=marks),
        in_specs=[pl.BlockSpec(memory_space=pltpu.SMEM)] + [anywhere] * 4,
        out_specs=[pl.BlockSpec(memory_space=pltpu.VMEM)] * len(widths),
        out_shape=[
            jax.ShapeDtypeStruct((dp, count, 2, rows, columns), near.dtype) for columns in widths
        ],
        scratch_shapes=[pltpu.SemaphoreType.DMA((8 * count * len(widths),))],
        compiler_params=pltpu.CompilerParams(vmem_limit_bytes=VMEM_BYTES),
        cost_estimate=pl.CostEstimate(flops=0, bytes_accessed=64 * near.size, transcendentals=0),
        name="assemble_rows",
    )(place, near, far, near_core, far_core)
    return [whole.reshape(-1, whole.shape[-1]) for whole in wholes]


def halves_kernel(*refs):
    *pieces, first, second = refs
    split = first.shape[2]
    for turn, piece in enumerate(pieces):
        first[turn] = piece[:, :split]
        second[turn] = piece[:, split:]


def halves(pieces, split):
    count, (rows, width) = len(pieces), pieces[0].shape
    vmem = pl.BlockSpec(memory_space=pltpu.VMEM)
    return pl.pallas_call(
        halves_kernel,
        in_specs=[vmem] * count,
        out_specs=[vmem] * 2,
        out_shape=[
            jax.ShapeDtypeStruct((count, rows, columns), pieces[0].dtype)
            for columns in (split, width - split)
        ],
        compiler_params=pltpu.CompilerParams(vmem_limit_bytes=VMEM_BYTES),
        name="stack_halves",
    )(*pieces)


def traded(pieces):
    return [pieces[0]] + [turned(piece, turn) for turn, piece in enumerate(pieces) if turn]


def turns(step):
    return (rank() + step * jnp.arange(ranks(), dtype=jnp.int32) + ranks()) % ranks()


def split_kernel(core_ref, rows_ref, own_ref, other_ref, *, block):
    for number in range(own_ref.shape[1] // block):
        there = slice(number * block, (number + 1) * block)
        for index, half_ref in ((core_ref[0], own_ref), (1 - core_ref[0], other_ref)):
            column = pl.multiple_of((2 * number + index) * block, block)
            half_ref[:, there] = rows_ref[:, pl.ds(column, block)]


def core_halves(rows):
    dp, (tokens, width) = lax.axis_size("dp"), rows.shape
    own = (lax.axis_index("dp") % 2).astype(jnp.int32).reshape(1)
    vmem = pl.BlockSpec(memory_space=pltpu.VMEM)
    return pl.pallas_call(
        functools.partial(split_kernel, block=width // dp),
        in_specs=[pl.BlockSpec(memory_space=pltpu.SMEM), vmem],
        out_specs=[vmem] * 2,
        out_shape=[jax.ShapeDtypeStruct((tokens, width // 2), rows.dtype)] * 2,
        compiler_params=pltpu.CompilerParams(vmem_limit_bytes=VMEM_BYTES),
        name="core_halves",
    )(own, rows)


def core_given(rows, grads):
    return outer_sum(rows[1], grads).astype(jnp.bfloat16)


def core_sum(rows, grads, got):
    dp, count = lax.axis_size("dp"), ranks()
    total = (outer_sum(rows[0], grads) + got.astype(jnp.float32)).astype(jnp.bfloat16)
    shape = (2,) * (len(dp_bits()) - 1) + (count, 2, total.shape[0] // (dp * count), total.shape[1])
    return total.reshape(shape)


def shrunk(state, route):
    terms, marks = state
    mark, exchange = route
    axis = marks.index(mark)
    own = (lax.axis_index("dp") // mark[0]) % 2 if mark[0] else side()
    got = exchange(pick(terms, 1 - own, axis))
    total = pick(terms, own, axis).astype(jnp.float32) + got.astype(jnp.float32)
    return (total.astype(jnp.bfloat16), marks[:axis] + marks[axis + 1 :])


def block_marks():
    return [(bit, 0) for bit in reversed(dp_bits()[1:])] + [None, (0, 1)]


def rank_groups():
    count = lax.axis_size("fsdp")
    return [list(range(here, count, 2)) for here in range(2)]


def reordered(blocks):
    return [pick(blocks, (rank() - number + ranks()) % ranks()) for number in range(ranks())]


def peers():
    dp, fsdp = lax.axis_size("dp"), lax.axis_size("fsdp")
    return [[d * fsdp + 2 * r + s for d in range(dp) for s in range(2)] for r in range(fsdp // 2)]


def peers_gather(rows):
    return lax.all_gather(rows, ("dp", "fsdp"), tiled=True, axis_index_groups=peers())


def peers_scatter(terms):
    return lax.psum_scatter(
        terms, ("dp", "fsdp"), scatter_dimension=0, tiled=True, axis_index_groups=peers()
    )


def matmul(left_side, right_side):
    return jnp.dot(left_side, right_side, preferred_element_type=jnp.float32)


def outer_sum(left_side, right_side):
    return lax.dot_general(left_side, right_side, TN, preferred_element_type=jnp.float32)


def back_product(left_side, right_side):
    return lax.dot_general(left_side, right_side, NT, preferred_element_type=jnp.float32)


def dot(left, right, dims, precision=HIGHEST):
    return lax.dot_general(
        left, right, dims, precision=precision, preferred_element_type=jnp.float32
    )


def decayed(forget_proj, slack, lower):
    sig = jax.nn.sigmoid(forget_proj)
    keys = slack * (1.0 - sig)
    running = dot(lower, jnp.log1p(-keys), NN)
    return (sig, keys, running)


def triangle(size):
    rows = lax.broadcasted_iota(jnp.int32, (size, size), 0)
    columns = lax.broadcasted_iota(jnp.int32, (size, size), 1)
    return jnp.where(rows >= columns, 1.0, 0.0)


def normed_head(mixed, gate):
    sig = jax.nn.sigmoid(gate)
    silu = gate * sig
    gated = mixed * silu
    centred = gated - jnp.mean(gated, axis=-1, keepdims=True)
    inv = lax.rsqrt(jnp.mean(centred * centred, axis=-1, keepdims=True) + 1e-05)
    return (sig, silu, inv, centred * inv)


def forward_kernel(
    order_ref, query_ref, value_ref, slack_ref, gain_ref, unit_ref, mixed_ref, states_ref, state
):
    span = query_ref.shape[1]
    share = slack_ref.shape[1]

    @pl.when(pl.program_id(0) == 0)
    def _():
        state[...] = jnp.zeros_like(state)

    states_ref[0] = state[...]
    lower = triangle(span)
    _, keys, running = decayed(query_ref[0, :, share:], slack_ref[...], lower)
    grown = jnp.exp(running)
    queries = query_ref[0, :, :share] * grown
    keys = keys * jnp.exp(-running)
    for head in range(share // HEAD):
        here = slice(head * HEAD, (head + 1) * HEAD)
        gate_here = slice(share + head * HEAD, share + (head + 1) * HEAD)
        values = value_ref[0, :, here]
        before = state[head]
        scores = dot(queries[:, here], keys[:, here], NT) * lower
        mixed = dot(scores, values, NN) + dot(queries[:, here], before, NT)
        state[head] = (before + dot(values, keys[:, here], TN)) * grown[span - 1 :, here]
        mixed_ref[0, :, here] = mixed
        normed = normed_head(mixed, value_ref[0, :, gate_here])[3]
        unit_ref[0, :, here] = (normed * gain_ref[:, here]).astype(jnp.bfloat16)


def backward_kernel(
    order_ref,
    query_ref,
    value_ref,
    slack_ref,
    gain_ref,
    mixed_ref,
    states_ref,
    d_unit_ref,
    d_query_ref,
    d_value_ref,
    term_ref,
    back,
    carry,
):
    span = query_ref.shape[1]
    share = slack_ref.shape[1]

    @pl.when(pl.program_id(0) == 0)
    def _():
        back[...] = jnp.zeros_like(back)
        carry[...] = jnp.zeros_like(carry)
        term_ref[...] = jnp.zeros_like(term_ref)

    lower = triangle(span)
    slack = slack_ref[...]
    sig, raw_keys, running = decayed(query_ref[0, :, share:], slack, lower)
    grown, shrunk = jnp.exp(running), jnp.exp(-running)
    all_queries = query_ref[0, :, :share] * grown
    all_keys = raw_keys * shrunk
    d_running, d_raw_keys = [], []
    for head in range(share // HEAD):
        here = slice(head * HEAD, (head + 1) * HEAD)
        there = slice(share + head * HEAD, share + (head + 1) * HEAD)
        queries, keys = all_queries[:, here], all_keys[:, here]
        values, gate = value_ref[0, :, here], value_ref[0, :, there]
        mixed = mixed_ref[0, :, here]
        d_unit = d_unit_ref[0, :, here]
        sig_gate, silu, inv, normed = normed_head(mixed, gate)
        term_ref[1:2, here] += jnp.sum(d_unit * normed, axis=0, keepdims=True)
        d_n = d_unit * gain_ref[:, here]
        d_gated = inv * (
            d_n
            - jnp.mean(d_n, axis=-1, keepdims=True)
            - normed * jnp.mean(d_n * normed, axis=-1, keepdims=True)
        )
        d_mixed = d_gated * silu
        d_gate = d_gated * mixed * sig_gate * (1.0 + gate * (1.0 - sig_gate))
        d_value_ref[0, :, there] = d_gate.astype(jnp.bfloat16)
        before = states_ref[0, head]
        after_grad = back[head] * grown[span - 1 :, here]
        scores = dot(queries, keys, NT) * lower
        d_scores = dot(d_mixed, values, NT) * lower
        d_queries = dot(d_scores, keys, NN) + dot(d_mixed, before, NN)
        d_keys = dot(d_scores, queries, TN) + dot(values, after_grad, NN)
        d_values = dot(scores, d_mixed, TN) + dot(keys, after_grad, NT)
        before_grad = dot(d_mixed, queries, TN) + after_grad
        d_value_ref[0, :, here] = d_values.astype(jnp.bfloat16)
        d_query_ref[0, :, here] = (d_queries * grown[:, here]).astype(jnp.bfloat16)
        back[head] = before_grad
        d_running.append(queries * d_queries - keys * d_keys)
        d_raw_keys.append(d_keys * shrunk[:, here])
    d_log = dot(lower, jnp.concatenate(d_running, axis=-1), TN) + carry[...]
    for head in range(share // HEAD):
        here = slice(head * HEAD, (head + 1) * HEAD)
        carry[:, here] = jnp.sum(states_ref[0, head] * back[head], axis=0, keepdims=True)
    e = jnp.concatenate(d_raw_keys, axis=-1) - d_log / (1.0 - raw_keys)
    term_ref[0:1, :] += jnp.sum(e * (1.0 - sig), axis=0, keepdims=True)
    d_query_ref[0, :, share:] = (-e * slack * sig * (1.0 - sig)).astype(jnp.bfloat16)


def row_block(step, order_ref):
    return (order_ref[step], 0, 0)


def state_block(step, order_ref):
    return (order_ref[step], 0, 0, 0)


def fixed_block(step, order_ref):
    return (0, 0)


def run_forward(order, queries, values, slack, gain):
    blocks, span, columns = queries.shape
    share = columns // 2
    heads = share // HEAD
    return pl.pallas_call(
        forward_kernel,
        grid_spec=pltpu.PrefetchScalarGridSpec(
            num_scalar_prefetch=1,
            grid=(blocks,),
            in_specs=[
                pl.BlockSpec((1, span, columns), row_block),
                pl.BlockSpec((1, span, columns), row_block),
                pl.BlockSpec((1, share), fixed_block),
                pl.BlockSpec((1, share), fixed_block),
            ],
            out_specs=[
                pl.BlockSpec((1, span, share), row_block),
                pl.BlockSpec((1, span, share), row_block),
                pl.BlockSpec((1, heads, HEAD, HEAD), state_block),
            ],
            scratch_shapes=[pltpu.VMEM((heads, HEAD, HEAD), jnp.float32)],
        ),
        out_shape=[
            jax.ShapeDtypeStruct((blocks, span, share), jnp.bfloat16),
            jax.ShapeDtypeStruct((blocks, span, share), jnp.float32),
            jax.ShapeDtypeStruct((blocks, heads, HEAD, HEAD), jnp.float32),
        ],
        compiler_params=pltpu.CompilerParams(vmem_limit_bytes=VMEM_BYTES),
        cost_estimate=pl.CostEstimate(
            flops=150 * queries.size * span, bytes_accessed=20 * queries.size, transcendentals=0
        ),
        name="recurrence_forward",
    )(order, queries, values, slack, gain)


def run_backward(order, queries, values, slack, gain, mixed, states, d_unit):
    blocks, span, columns = queries.shape
    share = columns // 2
    heads = share // HEAD
    return pl.pallas_call(
        backward_kernel,
        grid_spec=pltpu.PrefetchScalarGridSpec(
            num_scalar_prefetch=1,
            grid=(blocks,),
            in_specs=[
                pl.BlockSpec((1, span, columns), row_block),
                pl.BlockSpec((1, span, columns), row_block),
                pl.BlockSpec((1, share), fixed_block),
                pl.BlockSpec((1, share), fixed_block),
                pl.BlockSpec((1, span, share), row_block),
                pl.BlockSpec((1, heads, HEAD, HEAD), state_block),
                pl.BlockSpec((1, span, share), row_block),
            ],
            out_specs=[
                pl.BlockSpec((1, span, columns), row_block),
                pl.BlockSpec((1, span, columns), row_block),
                pl.BlockSpec((2, share), fixed_block),
            ],
            scratch_shapes=[
                pltpu.VMEM((heads, HEAD, HEAD), jnp.float32),
                pltpu.VMEM((1, share), jnp.float32),
            ],
        ),
        out_shape=[
            jax.ShapeDtypeStruct((blocks, span, columns), jnp.bfloat16),
            jax.ShapeDtypeStruct((blocks, span, columns), jnp.bfloat16),
            jax.ShapeDtypeStruct((2, share), jnp.float32),
        ],
        compiler_params=pltpu.CompilerParams(vmem_limit_bytes=VMEM_BYTES),
        cost_estimate=pl.CostEstimate(
            flops=250 * queries.size * span, bytes_accessed=30 * queries.size, transcendentals=0
        ),
        name="recurrence_backward",
    )(order, queries, values, slack, gain, mixed, states, d_unit)


def inverse_rms(values):
    return lax.rsqrt(jnp.mean(values * values, axis=-1, keepdims=True) + 1e-06)


def unscaled_grad(d_scaled, scaled, inverse):
    return inverse * (d_scaled - scaled * jnp.mean(d_scaled * scaled, axis=-1, keepdims=True))


def on_device(
    inputs,
    cotangent,
    norm_gain,
    mixer_gain,
    ffn_gain,
    slack,
    w_query,
    w_forget,
    w_input,
    w_gate_out,
    w_out,
    w_gate,
    w_up,
    w_down,
):
    width = inputs.shape[-1]
    dp, count, here = lax.axis_size("dp"), ranks(), rank()
    float32, bfloat16 = jnp.float32, jnp.bfloat16
    sending, taking = turns(1), turns(-1)
    mixer_weights = (w_query, w_forget, w_input, w_gate_out)
    ffn_weights = (w_gate, w_up)
    core, big = 1, dp // 2
    in_place = 2 * w_out.shape[0] == HEAD
    chunks = dp if in_place else 1

    def to_rank(rows):
        return rows if in_place else to_users(rows)

    def from_rank(rows):
        return rows if in_place else to_owners(rows)

    gains = jnp.stack([norm_gain, ffn_gain, mixer_gain, slack], axis=1)
    gains = jnp.pad(gains, ((0, 0), (0, LANES - gains.shape[1])))
    cut = traded(cut_columns(sending, (w_query, w_forget, gains, w_input, w_gate_out), chunks))
    own_in, own_d = to_side(inputs, cotangent)
    mixer_out = peers_gather(to_rank(w_out))
    own_in, own_d, cut = sync(own_in, own_d, cut)

    by_big, by_side = ((big, 0), functools.partial(across, bit=big)), ((0, 1), swapped)
    first_in = gather_first(own_in)
    split = 2 * (width // count) + LANES
    query_cut, value_cut = halves(cut, split)
    query_near = jnp.stack([query_cut, across(query_cut, big)])
    value_near = jnp.stack([value_cut, swapped(value_cut)])
    cut = cut_columns(sending, (w_gate, w_up), chunks)
    first_in, query_near, value_near, own_d, cut, mixer_out = sync(
        first_in, query_near, value_near, own_d, cut, mixer_out
    )

    second_in = gather_second(first_in)
    query_far = swapped(query_near)
    value_far = across(value_near, big)
    waiting = list(cut[1:])
    cut = [cut[0], turned(waiting[0], 1)]
    second_in, query_far, value_far, cut, waiting, own_d = sync(
        second_in, query_far, value_far, cut, waiting, own_d
    )

    query_blocks = (query_near, query_far, across(query_near, core), across(query_far, core))
    value_blocks = (value_near, value_far, across(value_near, core), across(value_far, core))
    raw_in = gathered(own_in, first_in, second_in)
    raw_in, query_blocks, value_blocks, cut, waiting, own_d, late_down = sync(
        raw_in, query_blocks, value_blocks, cut, waiting, own_d, w_down
    )

    down = peers_gather(to_rank(late_down))
    for turn in range(2, count):
        cut = cut + [turned(waiting[turn - 1], turn)]
    share = 2 * (width // count)
    query_in, gains = assembled(*query_blocks, False, (share, LANES))
    (value_in,) = assembled(*value_blocks, True, (share,))
    gains = jnp.transpose(gains)[:4].astype(float32)
    gain_first, gain_second = gains[0], gains[1]
    here_gains = pick(gains.reshape(4, chunks, count, -1), here, 2).reshape(4, -1)[2:]
    mixer_gain_here, slack_here = here_gains[:1], here_gains[1:]
    all_tokens = raw_in.astype(float32)
    rows_in = (all_tokens * inverse_rms(all_tokens) * gain_first).astype(bfloat16)
    queries = matmul(rows_in, query_in).reshape(count, -1, share)
    values = matmul(rows_in, value_in).reshape(count, -1, share)
    queries, values, cut = sync(queries, values, cut)

    units = cut[0].shape[-1] // 2
    gate_cut, up_cut = halves(cut, units)
    gate_near, up_near = across(gate_cut, big), swapped(up_cut)
    unit, mixed, states = run_forward(taking, queries, values, slack_here, mixer_gain_here)
    unit, mixed, states, gate_near, up_near = sync(unit, mixed, states, gate_near, up_near)
    gate_near, up_near = jnp.stack([gate_cut, gate_near]), jnp.stack([up_cut, up_near])
    rows_unit = unit.reshape(-1, unit.shape[-1])
    branch_terms = by_turn(matmul(away_rows(rows_unit), mixer_out))
    branch_terms, gate_near, up_near, own_d = sync(branch_terms, gate_near, up_near, own_d)

    branch_first = scatter_first(branch_terms)
    branch_own = matmul(own_rows(rows_unit), mixer_out)
    gate_far = swapped(gate_near)
    up_far = across(up_near, big)
    rows_d = lax.all_gather(own_d, "fsdp", axis_index_groups=rank_groups())
    branch_first, branch_own, gate_near, up_near, gate_far, up_far, branch_terms = sync(
        branch_first, branch_own, gate_near, up_near, gate_far, up_far, branch_terms
    )

    branch_second = scatter_second(branch_terms, branch_first)
    gate_blocks = (gate_near, gate_far, across(gate_near, core))
    up_blocks = (up_near, up_far, across(up_near, core))
    tokens = own_in.astype(float32)
    hidden = tokens + scattered(branch_own, branch_first, branch_second)
    second_inverse = inverse_rms(hidden)
    hidden_hat = hidden * second_inverse
    own_mid = (hidden_hat * gain_second).astype(bfloat16)
    own_mid, gate_blocks, up_blocks, down = sync(own_mid, gate_blocks, up_blocks, down)

    all_mid = gather_first(own_mid, False)
    gate_blocks = gate_blocks + (across(gate_blocks[1], core),)
    up_blocks = up_blocks + (across(up_blocks[1], core),)
    (gate_in,) = assembled(*gate_blocks, False, (units,))
    (up_in,) = assembled(*up_blocks, True, (units,))
    all_mid, rows_d, gate_in, up_in = sync(all_mid, rows_d, gate_in, up_in)

    rows_mid = gathered_directly(own_mid, all_mid)
    gate_proj = matmul(rows_mid, gate_in)
    up_proj = matmul(rows_mid, up_in)
    rows_d = jnp.concatenate(reordered(rows_d), axis=0)
    sig = jax.nn.sigmoid(gate_proj)
    inner = (gate_proj * sig * up_proj).astype(bfloat16)
    d_inner = back_product(rows_d, down)
    d_gate = (d_inner * up_proj * sig * (1.0 + gate_proj * (1.0 - sig))).astype(bfloat16)
    d_up = (d_inner * gate_proj * sig).astype(bfloat16)

    def hidden_product(cut):
        return back_product(cut(d_gate), gate_in) + back_product(cut(d_up), up_in)

    mid_terms = by_turn(hidden_product(away_rows))
    mid_terms, d_gate, d_up, inner = sync(mid_terms, d_gate, d_up, inner)

    mid_first = scatter_first(mid_terms)
    mid_own = hidden_product(own_rows)
    halves_mid = core_halves(rows_mid)
    gate_given, up_given = core_given(halves_mid, d_gate), core_given(halves_mid, d_up)
    mid_first, mid_own, mid_terms, halves_mid, inner, gate_given, up_given = sync(
        mid_first, mid_own, mid_terms, halves_mid, inner, gate_given, up_given
    )

    mid_second = scatter_second(mid_terms, mid_first)
    gate_got, up_got = across(gate_given, core), across(up_given, core)
    marks = block_marks()
    d_hidden = own_d.astype(float32) + unscaled_grad(
        scattered(mid_own, mid_first, mid_second) * gain_second, hidden_hat, second_inverse
    )
    own_branch, gate_got, up_got, inner, halves_mid = sync(
        d_hidden.astype(bfloat16), gate_got, up_got, inner, halves_mid
    )

    all_branch = gather_first(own_branch, False)
    gate_total = core_sum(halves_mid, d_gate, gate_got)
    up_total = core_sum(halves_mid, d_up, up_got)
    gate_total, gate_marks = shrunk((gate_total, marks), by_side)
    up_total, up_marks = shrunk((up_total, marks), by_big)
    out_part = matmul(inner, down).astype(bfloat16).reshape(count, -1, width)
    out_part = jnp.stack(reordered(out_part))
    down_term = outer_sum(inner, rows_d).astype(bfloat16)
    halves_in = core_halves(rows_in)
    all_branch, gate_total, up_total, out_part, halves_in, down_term = sync(
        all_branch, gate_total, up_total, out_part, halves_in, down_term
    )

    out_part = lax.psum_scatter(
        out_part, "fsdp", scatter_dimension=0, axis_index_groups=rank_groups()
    )
    gate_total, _ = shrunk((gate_total, gate_marks), by_big)
    up_total, _ = shrunk((up_total, up_marks), by_side)

    def parts(*totals):
        picked = [[pick(total, sending[turn]) for total in totals] for turn in range(count)]
        return [jnp.concatenate(pieces, axis=-1) for pieces in picked]

    rows_branch = gathered_directly(own_branch, all_branch)
    d_unit = back_product(rows_branch, mixer_out).reshape(count, -1, mixer_out.shape[0])
    d_queries, d_values, terms = run_backward(
        taking[::-1], queries, values, slack_here, mixer_gain_here, mixed, states, d_unit
    )
    d_queries, d_values, terms, gate_total, up_total = sync(
        d_queries, d_values, terms, gate_total, up_total
    )
    d_queries = d_queries.reshape(-1, share)
    d_values = d_values.reshape(-1, share)

    def token_product(cut):
        return back_product(cut(d_queries), query_in) + back_product(cut(d_values), value_in)

    in_terms = by_turn(token_product(away_rows))
    waiting = parts(gate_total, up_total)
    in_terms, d_queries, d_values, terms, waiting, down_term = sync(
        in_terms, d_queries, d_values, terms, waiting, down_term
    )

    in_first = scatter_first(in_terms)
    query_total = core_sum(halves_in, d_queries, across(core_given(halves_in, d_queries), core))
    value_total = core_sum(halves_in, d_values, across(core_given(halves_in, d_values), core))
    in_own = token_product(own_rows)
    terms = terms + across(terms, core)
    in_first, in_own, query_total, value_total, terms, in_terms, rows_branch, waiting, out_part = sync(
        in_first, in_own, query_total, value_total, terms, in_terms, rows_branch, waiting, out_part
    )

    in_second = scatter_second(in_terms, in_first)
    query_next, query_marks = shrunk((query_total, marks), by_side)
    value_next, value_marks = shrunk((value_total, marks), by_big)
    out_term = outer_sum(rows_unit, rows_branch).astype(bfloat16)
    peer_terms = [term.reshape(2 * dp, -1, width) for term in (out_term, down_term)]
    peer_sum = peers_scatter(jnp.concatenate(peer_terms, axis=1).reshape(-1, width))
    ffn_parts = [waiting[0], turned(waiting[1], 1)]
    in_second, query_total, value_total, terms, ffn_parts, waiting = sync(
        in_second, query_next, value_next, terms, ffn_parts, waiting
    )

    ffn_parts = ffn_parts + [turned(waiting[turn], turn) for turn in range(2, count)]

    query_total, _ = shrunk((query_total, query_marks), by_big)
    value_total, _ = shrunk((value_total, value_marks), by_side)
    terms = terms + swapped(terms)
    first_inverse = inverse_rms(tokens)
    d_normed = scattered(in_own, in_first, in_second)
    input_grad = d_hidden + unscaled_grad(
        d_normed * gain_first, tokens * first_inverse, first_inverse
    )
    output = hidden + out_part.astype(float32)
    query_total, value_total, terms, input_grad, output, ffn_parts = sync(
        query_total, value_total, terms, input_grad, output, ffn_parts
    )

    waiting = parts(query_total, value_total)
    mixer_parts = [waiting[0]] + [turned(waiting[turn], turn) for turn in range(1, count)]
    ffn_parts, mixer_first = sync(ffn_parts, mixer_parts[1])
    mixer_parts = mixer_parts[:1] + [mixer_first] + mixer_parts[2:]
    grads_ffn, ffn_product = join_columns(taking, ffn_parts, ffn_weights, chunks)
    out_rows = w_out.shape[0]
    grad_out, grad_down = from_rank(peer_sum[:out_rows]), from_rank(peer_sum[out_rows:])
    output, input_grad = from_side(output, input_grad)
    terms = terms + across(terms, big)
    terms = from_rank(pick(terms.reshape(2, 2 * dp, -1), 2 * lax.axis_index("dp") + side(), 1))
    mixer_parts, ffn_product = sync(mixer_parts, ffn_product)
    grads_mixer, mixer_product = join_columns(taking, mixer_parts, mixer_weights, chunks)

    return (
        output,
        input_grad,
        mixer_product / norm_gain.astype(float32),
        terms[1],
        ffn_product / ffn_gain.astype(float32),
        terms[0],
        *grads_mixer,
        grad_out.astype(float32),
        *grads_ffn,
        grad_down.astype(float32),
    )


def solution(mesh):
    in_specs = (
        P(None, "dp", "fsdp", None),
        P(None, "dp", "fsdp", None),
        P(("dp", "fsdp")),
        P(("dp", "fsdp")),
        P(("dp", "fsdp")),
        P(("dp", "fsdp")),
        P(("dp", "fsdp"), None),
        P(("dp", "fsdp"), None),
        P(("dp", "fsdp"), None),
        P(("dp", "fsdp"), None),
        P(("dp", "fsdp"), None),
        P(("dp", "fsdp"), None),
        P(("dp", "fsdp"), None),
        P(("dp", "fsdp"), None),
    )
    out_specs = (
        P(None, "dp", "fsdp", None),
        P(None, "dp", "fsdp", None),
        P(("dp", "fsdp")),
        P(("dp", "fsdp")),
        P(("dp", "fsdp")),
        P(("dp", "fsdp")),
        P(("dp", "fsdp"), None),
        P(("dp", "fsdp"), None),
        P(("dp", "fsdp"), None),
        P(("dp", "fsdp"), None),
        P(("dp", "fsdp"), None),
        P(("dp", "fsdp"), None),
        P(("dp", "fsdp"), None),
        P(("dp", "fsdp"), None),
    )
    return jax.shard_map(
        on_device, mesh=mesh, in_specs=in_specs, out_specs=out_specs, check_vma=False
    )
```

```python
import functools

import jax
import jax.numpy as jnp
from jax import lax
from jax.experimental import pallas as pl
from jax.experimental.pallas import tpu as pltpu
from jax.sharding import PartitionSpec as P

HEAD = 128
LANES = 128
VMEM_BYTES = 56 * 1024 * 1024
HIGHEST = lax.Precision.HIGHEST
NN = (((1,), (0,)), ((), ()))
NT = (((1,), (1,)), ((), ()))
TN = (((0,), (0,)), ((), ()))


def ranks():
    return lax.axis_size("fsdp") // 2


def rank():
    return lax.axis_index("fsdp") // 2


def side():
    return lax.axis_index("fsdp") % 2


def pick(array, index, axis=0):
    return lax.dynamic_index_in_dim(array, index, axis, False)


def swapped(array):
    count = lax.axis_size("fsdp")
    return lax.ppermute(array, "fsdp", [(i, i ^ 1) for i in range(count)])


def turned(array, turn):
    count = lax.axis_size("fsdp")
    return lax.ppermute(array, "fsdp", [(i, (i + 2 * turn) % count) for i in range(count)])


def across(array, bit):
    count = lax.axis_size("dp")
    return lax.ppermute(array, "dp", [(i, i ^ bit) for i in range(count)])


def placed(pieces):
    whole = jnp.zeros((len(pieces),) + pieces[0][1].shape, pieces[0][1].dtype)
    for index, piece in pieces:
        whole = lax.dynamic_update_index_in_dim(whole, piece, index, 0)
    return whole


def to_side(*arrays):
    here = side()
    got = swapped(jnp.concatenate([pick(array, 1 - here) for array in arrays], axis=0))
    both = [placed([(here, pick(a, here)[0]), (1 - here, piece)]) for a, piece in zip(arrays, got)]
    return [rows.reshape((-1,) + rows.shape[2:]) for rows in both]


def from_side(*arrays):
    here = side()
    halves = [rows.reshape((2, 1, rows.shape[0] // 2) + rows.shape[1:]) for rows in arrays]
    got = swapped(jnp.concatenate([pick(half, 1 - here) for half in halves], axis=0))
    return [
        placed([(here, pick(half, here)), (1 - here, piece[None])]) for half, piece in zip(halves, got)
    ]


def shifted(array, step, among=None):
    count = ranks()
    starts = [r for r in (range(count) if among is None else among) if 0 <= r + step < count]
    moves = [(2 * r + s, 2 * (r + step) + s) for r in starts for s in range(2)]
    return lax.ppermute(array, "fsdp", moves)


def ends_traded(array):
    last = lax.axis_size("fsdp") - 2
    moves = [(s, last + s) for s in range(2)] + [(last + s, s) for s in range(2)]
    return lax.ppermute(array, "fsdp", moves)


def gather_first(own, relay=True):
    if ranks() != 4 or not relay:
        return [turned(own, turn) for turn in range(1, ranks())]
    return [shifted(own, 1), shifted(own, -1), ends_traded(own)]


def gather_second(first):
    return [] if ranks() != 4 else [shifted(first[0], 1, (1, 2)), shifted(first[1], -1, (1, 2))]


def gathered_directly(own, pieces):
    return jnp.concatenate([own] + pieces, axis=0)


def gathered(own, first, second):
    here = rank()
    if ranks() != 4:
        return jnp.concatenate([own] + first, axis=0)
    up, down, ends = first
    up2, down2 = second
    near = [jnp.where(here == 0, ends, up), jnp.where(here >= 2, up2, down2)]
    return jnp.concatenate([own] + near + [jnp.where(here == 3, ends, down)], axis=0)


def away_rows(operand):
    return operand[operand.shape[0] // ranks() :]


def own_rows(operand):
    return operand[: operand.shape[0] // ranks()]


def by_turn(away):
    return jnp.split(away.astype(jnp.bfloat16), ranks() - 1, axis=0)


def scatter_first(terms):
    if ranks() != 4:
        return [turned(term, -turn - 1) for turn, term in enumerate(terms)]
    ends = jnp.where(rank() == 0, terms[0], terms[2])
    return [shifted(terms[1], 1, (0, 1)), shifted(terms[1], -1, (2, 3)), ends_traded(ends)]


def scatter_second(terms, first):
    if ranks() != 4:
        return []
    up = terms[2].astype(jnp.float32) + first[0].astype(jnp.float32)
    down = terms[0].astype(jnp.float32) + first[1].astype(jnp.float32)
    return [shifted(up.astype(jnp.bfloat16), 1), shifted(down.astype(jnp.bfloat16), -1)]


def scattered(own, first, second):
    for piece in first if ranks() != 4 else first[2:] + second:
        own = own + piece.astype(jnp.float32)
    return own


def sync(*arrays):
    return lax.optimization_barrier(arrays)


def dp_bits():
    bits, bit = [], 1
    while bit < lax.axis_size("dp"):
        bits.append(bit)
        bit *= 2
    return bits


def routes(side_first):
    bits = [((bit, 0), functools.partial(across, bit=bit)) for bit in reversed(dp_bits())]
    return [((0, 1), swapped)] + bits if side_first else bits[:-1] + [((0, 1), swapped)] + bits[-1:]


def user_moves():
    dp, fsdp = lax.axis_size("dp"), lax.axis_size("fsdp")
    moves = []
    for block in range(dp * fsdp):
        user, part = divmod(block, 2 * dp)
        moves.append((block, (part // 2) * fsdp + 2 * user + part % 2))
    return moves


def to_users(rows):
    return lax.ppermute(rows, ("dp", "fsdp"), user_moves())


def to_owners(rows):
    return lax.ppermute(rows, ("dp", "fsdp"), [(b, a) for a, b in user_moves()])


def for_rank(wanted, body, aligned):
    if aligned:
        body(wanted)
        return
    for number in range(ranks()):
        pl.when(wanted == number)(functools.partial(body, number))


def columns_of(number, chunk, weight, chunks, count):
    width = weight.shape[1] // (chunks * count)
    start = chunk * (weight.shape[1] // chunks) + number * width
    return pl.ds(start if isinstance(number, int) else pl.multiple_of(start, LANES), width)


def cut_kernel(order_ref, *refs, chunks):
    count = order_ref.shape[0]
    weights, pieces = refs[:-count], refs[-count:]
    for turn in range(count):

        def cut(number, turn=turn):
            start = 0
            for weight in weights:
                if weight.shape[1] == LANES:
                    pieces[turn][:, start : start + LANES] = weight[...]
                    start += LANES
                    continue
                for chunk in range(chunks):
                    columns = columns_of(number, chunk, weight, chunks, count)
                    pieces[turn][:, start : start + columns.size] = weight[:, columns]
                    start += columns.size

        widths = [w.shape[1] // (chunks * count) for w in weights if w.shape[1] != LANES]
        for_rank(order_ref[turn], cut, all(width % LANES == 0 for width in widths))


def cut_columns(order, weights, chunks):
    count = ranks()
    rows = weights[0].shape[0]
    vmem = pl.BlockSpec(memory_space=pltpu.VMEM)
    width = sum(LANES if w.shape[1] == LANES else w.shape[1] // count for w in weights)
    return pl.pallas_call(
        functools.partial(cut_kernel, chunks=chunks),
        in_specs=[pl.BlockSpec(memory_space=pltpu.SMEM)] + [vmem] * len(weights),
        out_specs=[vmem] * count,
        out_shape=[jax.ShapeDtypeStruct((rows, width), weights[0].dtype)] * count,
        compiler_params=pltpu.CompilerParams(vmem_limit_bytes=VMEM_BYTES),
        name="cut_columns",
    )(order, *weights)


def join_kernel(order_ref, *refs, chunks):
    count = order_ref.shape[0]
    parts = (len(refs) - count - 1) // 2
    pieces, weights = refs[:count], refs[count : count + parts]
    grads, product = refs[count + parts : -1], refs[-1]
    product[...] = jnp.zeros(product.shape, jnp.float32)
    for turn in range(count):

        def join(number, turn=turn):
            start = 0
            total = jnp.zeros(product.shape, jnp.float32)
            for weight, grad in zip(weights, grads):
                for chunk in range(chunks):
                    columns = columns_of(number, chunk, weight, chunks, count)
                    piece = pieces[turn][:, start : start + columns.size].astype(jnp.float32)
                    grad[:, columns] = piece
                    term = piece * weight[:, columns].astype(jnp.float32)
                    total = total + jnp.sum(term, axis=1, keepdims=True)
                    start += columns.size
            product[...] += total

        widths = [w.shape[1] // (chunks * count) for w in weights]
        for_rank(order_ref[turn], join, all(width % LANES == 0 for width in widths))


def join_columns(order, pieces, weights, chunks):
    rows = weights[0].shape[0]
    vmem = pl.BlockSpec(memory_space=pltpu.VMEM)
    *grads, product = pl.pallas_call(
        functools.partial(join_kernel, chunks=chunks),
        in_specs=[pl.BlockSpec(memory_space=pltpu.SMEM)] + [vmem] * (len(pieces) + len(weights)),
        out_specs=[vmem] * (len(weights) + 1),
        out_shape=[jax.ShapeDtypeStruct(w.shape, jnp.float32) for w in weights]
        + [jax.ShapeDtypeStruct((rows, 1), jnp.float32)],
        compiler_params=pltpu.CompilerParams(vmem_limit_bytes=VMEM_BYTES),
        cost_estimate=pl.CostEstimate(
            flops=0, bytes_accessed=40 * sum(w.size for w in weights), transcendentals=0
        ),
        name="join_columns",
    )(order, *pieces, *weights)
    return grads, product[:, 0]


def assemble_kernel(place_ref, *refs, marks):
    (*blocks, sems), wholes = refs[:4] + refs[-1:], refs[4:-1]
    count = blocks[0].shape[1]
    dp_index, here, first_rank = place_ref[0], place_ref[1], place_ref[2]
    copies = []
    for core in range(2):
        for outer in range(2):
            block = blocks[2 * core + outer]
            for inner in range(2):
                dp_mark, side_mark = marks[outer][inner]
                spot = jnp.bitwise_xor(dp_index, dp_mark + core)
                its_side = jnp.bitwise_xor(here, side_mark)
                for turn in range(count):
                    its_rank = lax.rem(first_rank - turn + count, count)
                    start = 0
                    for whole in wholes:
                        columns = whole.shape[-1]
                        source = block.at[inner, turn, :, pl.ds(start, columns)]
                        target = whole.at[spot, its_rank, its_side]
                        copies.append(pltpu.make_async_copy(source, target, sems.at[len(copies)]))
                        copies[-1].start()
                        start += columns
    for copy in copies:
        copy.wait()


def assembled(near, far, near_core, far_core, side_first, widths):
    dp, (_, count, rows, _) = lax.axis_size("dp"), near.shape
    big = dp // 2
    marks = (((0, 0), (0, 1)), ((big, 0), (big, 1))) if side_first else (((0, 0), (big, 0)), ((0, 1), (big, 1)))
    place = jnp.stack([lax.axis_index("dp"), side(), rank()]).astype(jnp.int32)
    anywhere = pl.BlockSpec(memory_space=pl.ANY)
    wholes = pl.pallas_call(
        functools.partial(assemble_kernel, marks=marks),
        in_specs=[pl.BlockSpec(memory_space=pltpu.SMEM)] + [anywhere] * 4,
        out_specs=[pl.BlockSpec(memory_space=pltpu.VMEM)] * len(widths),
        out_shape=[
            jax.ShapeDtypeStruct((dp, count, 2, rows, columns), near.dtype) for columns in widths
        ],
        scratch_shapes=[pltpu.SemaphoreType.DMA((8 * count * len(widths),))],
        compiler_params=pltpu.CompilerParams(vmem_limit_bytes=VMEM_BYTES),
        cost_estimate=pl.CostEstimate(flops=0, bytes_accessed=64 * near.size, transcendentals=0),
        name="assemble_rows",
    )(place, near, far, near_core, far_core)
    return [whole.reshape(-1, whole.shape[-1]) for whole in wholes]


def halves_kernel(*refs):
    *pieces, first, second = refs
    split = first.shape[2]
    for turn, piece in enumerate(pieces):
        first[turn] = piece[:, :split]
        second[turn] = piece[:, split:]


def halves(pieces, split):
    count, (rows, width) = len(pieces), pieces[0].shape
    vmem = pl.BlockSpec(memory_space=pltpu.VMEM)
    return pl.pallas_call(
        halves_kernel,
        in_specs=[vmem] * count,
        out_specs=[vmem] * 2,
        out_shape=[
            jax.ShapeDtypeStruct((count, rows, columns), pieces[0].dtype)
            for columns in (split, width - split)
        ],
        compiler_params=pltpu.CompilerParams(vmem_limit_bytes=VMEM_BYTES),
        name="stack_halves",
    )(*pieces)


def traded(pieces):
    return [pieces[0]] + [turned(piece, turn) for turn, piece in enumerate(pieces) if turn]


def turns(step):
    return (rank() + step * jnp.arange(ranks(), dtype=jnp.int32) + ranks()) % ranks()


def split_kernel(core_ref, rows_ref, own_ref, other_ref, *, block):
    for number in range(own_ref.shape[1] // block):
        there = slice(number * block, (number + 1) * block)
        for index, half_ref in ((core_ref[0], own_ref), (1 - core_ref[0], other_ref)):
            column = pl.multiple_of((2 * number + index) * block, block)
            half_ref[:, there] = rows_ref[:, pl.ds(column, block)]


def core_halves(rows):
    dp, (tokens, width) = lax.axis_size("dp"), rows.shape
    own = (lax.axis_index("dp") % 2).astype(jnp.int32).reshape(1)
    vmem = pl.BlockSpec(memory_space=pltpu.VMEM)
    return pl.pallas_call(
        functools.partial(split_kernel, block=width // dp),
        in_specs=[pl.BlockSpec(memory_space=pltpu.SMEM), vmem],
        out_specs=[vmem] * 2,
        out_shape=[jax.ShapeDtypeStruct((tokens, width // 2), rows.dtype)] * 2,
        compiler_params=pltpu.CompilerParams(vmem_limit_bytes=VMEM_BYTES),
        name="core_halves",
    )(own, rows)


def core_given(rows, grads):
    return outer_sum(rows[1], grads).astype(jnp.bfloat16)


def core_sum(rows, grads, got):
    dp, count = lax.axis_size("dp"), ranks()
    total = (outer_sum(rows[0], grads) + got.astype(jnp.float32)).astype(jnp.bfloat16)
    shape = (2,) * (len(dp_bits()) - 1) + (count, 2, total.shape[0] // (dp * count), total.shape[1])
    return total.reshape(shape)


def shrunk(state, route):
    terms, marks = state
    mark, exchange = route
    axis = marks.index(mark)
    own = (lax.axis_index("dp") // mark[0]) % 2 if mark[0] else side()
    got = exchange(pick(terms, 1 - own, axis))
    total = pick(terms, own, axis).astype(jnp.float32) + got.astype(jnp.float32)
    return (total.astype(jnp.bfloat16), marks[:axis] + marks[axis + 1 :])


def block_marks():
    return [(bit, 0) for bit in reversed(dp_bits()[1:])] + [None, (0, 1)]


def rank_groups():
    count = lax.axis_size("fsdp")
    return [list(range(here, count, 2)) for here in range(2)]


def reordered(blocks):
    return [pick(blocks, (rank() - number + ranks()) % ranks()) for number in range(ranks())]


def peers():
    dp, fsdp = lax.axis_size("dp"), lax.axis_size("fsdp")
    return [[d * fsdp + 2 * r + s for d in range(dp) for s in range(2)] for r in range(fsdp // 2)]


def peers_gather(rows):
    return lax.all_gather(rows, ("dp", "fsdp"), tiled=True, axis_index_groups=peers())


def peers_scatter(terms):
    return lax.psum_scatter(
        terms, ("dp", "fsdp"), scatter_dimension=0, tiled=True, axis_index_groups=peers()
    )


def matmul(left_side, right_side):
    return jnp.dot(left_side, right_side, preferred_element_type=jnp.float32)


def outer_sum(left_side, right_side):
    return lax.dot_general(left_side, right_side, TN, preferred_element_type=jnp.float32)


def back_product(left_side, right_side):
    return lax.dot_general(left_side, right_side, NT, preferred_element_type=jnp.float32)


def dot(left, right, dims, precision=HIGHEST):
    return lax.dot_general(
        left, right, dims, precision=precision, preferred_element_type=jnp.float32
    )


def decayed(forget_proj, slack, lower):
    sig = jax.nn.sigmoid(forget_proj)
    keys = slack * (1.0 - sig)
    running = dot(lower, jnp.log1p(-keys), NN)
    return (sig, keys, running)


def triangle(size):
    rows = lax.broadcasted_iota(jnp.int32, (size, size), 0)
    columns = lax.broadcasted_iota(jnp.int32, (size, size), 1)
    return jnp.where(rows >= columns, 1.0, 0.0)


def normed_head(mixed, gate):
    sig = jax.nn.sigmoid(gate)
    silu = gate * sig
    gated = mixed * silu
    centred = gated - jnp.mean(gated, axis=-1, keepdims=True)
    inv = lax.rsqrt(jnp.mean(centred * centred, axis=-1, keepdims=True) + 1e-05)
    return (sig, silu, inv, centred * inv)


def forward_kernel(
    order_ref, query_ref, value_ref, slack_ref, gain_ref, unit_ref, mixed_ref, states_ref, state
):
    span = query_ref.shape[1]
    share = slack_ref.shape[1]

    @pl.when(pl.program_id(0) == 0)
    def _():
        state[...] = jnp.zeros_like(state)

    states_ref[0] = state[...]
    lower = triangle(span)
    _, keys, running = decayed(query_ref[0, :, share:], slack_ref[...], lower)
    grown = jnp.exp(running)
    queries = query_ref[0, :, :share] * grown
    keys = keys * jnp.exp(-running)
    for head in range(share // HEAD):
        here = slice(head * HEAD, (head + 1) * HEAD)
        gate_here = slice(share + head * HEAD, share + (head + 1) * HEAD)
        values = value_ref[0, :, here]
        before = state[head]
        scores = dot(queries[:, here], keys[:, here], NT) * lower
        mixed = dot(scores, values, NN) + dot(queries[:, here], before, NT)
        state[head] = (before + dot(values, keys[:, here], TN)) * grown[span - 1 :, here]
        mixed_ref[0, :, here] = mixed
        normed = normed_head(mixed, value_ref[0, :, gate_here])[3]
        unit_ref[0, :, here] = (normed * gain_ref[:, here]).astype(jnp.bfloat16)


def backward_kernel(
    order_ref,
    query_ref,
    value_ref,
    slack_ref,
    gain_ref,
    mixed_ref,
    states_ref,
    d_unit_ref,
    d_query_ref,
    d_value_ref,
    term_ref,
    back,
    carry,
):
    span = query_ref.shape[1]
    share = slack_ref.shape[1]

    @pl.when(pl.program_id(0) == 0)
    def _():
        back[...] = jnp.zeros_like(back)
        carry[...] = jnp.zeros_like(carry)
        term_ref[...] = jnp.zeros_like(term_ref)

    lower = triangle(span)
    slack = slack_ref[...]
    sig, raw_keys, running = decayed(query_ref[0, :, share:], slack, lower)
    grown, shrunk = jnp.exp(running), jnp.exp(-running)
    all_queries = query_ref[0, :, :share] * grown
    all_keys = raw_keys * shrunk
    d_running, d_raw_keys = [], []
    for head in range(share // HEAD):
        here = slice(head * HEAD, (head + 1) * HEAD)
        there = slice(share + head * HEAD, share + (head + 1) * HEAD)
        queries, keys = all_queries[:, here], all_keys[:, here]
        values, gate = value_ref[0, :, here], value_ref[0, :, there]
        mixed = mixed_ref[0, :, here]
        d_unit = d_unit_ref[0, :, here]
        sig_gate, silu, inv, normed = normed_head(mixed, gate)
        term_ref[1:2, here] += jnp.sum(d_unit * normed, axis=0, keepdims=True)
        d_n = d_unit * gain_ref[:, here]
        d_gated = inv * (
            d_n
            - jnp.mean(d_n, axis=-1, keepdims=True)
            - normed * jnp.mean(d_n * normed, axis=-1, keepdims=True)
        )
        d_mixed = d_gated * silu
        d_gate = d_gated * mixed * sig_gate * (1.0 + gate * (1.0 - sig_gate))
        d_value_ref[0, :, there] = d_gate.astype(jnp.bfloat16)
        before = states_ref[0, head]
        after_grad = back[head] * grown[span - 1 :, here]
        scores = dot(queries, keys, NT) * lower
        d_scores = dot(d_mixed, values, NT) * lower
        d_queries = dot(d_scores, keys, NN) + dot(d_mixed, before, NN)
        d_keys = dot(d_scores, queries, TN) + dot(values, after_grad, NN)
        d_values = dot(scores, d_mixed, TN) + dot(keys, after_grad, NT)
        before_grad = dot(d_mixed, queries, TN) + after_grad
        d_value_ref[0, :, here] = d_values.astype(jnp.bfloat16)
        d_query_ref[0, :, here] = (d_queries * grown[:, here]).astype(jnp.bfloat16)
        back[head] = before_grad
        d_running.append(queries * d_queries - keys * d_keys)
        d_raw_keys.append(d_keys * shrunk[:, here])
    d_log = dot(lower, jnp.concatenate(d_running, axis=-1), TN) + carry[...]
    for head in range(share // HEAD):
        here = slice(head * HEAD, (head + 1) * HEAD)
        carry[:, here] = jnp.sum(states_ref[0, head] * back[head], axis=0, keepdims=True)
    e = jnp.concatenate(d_raw_keys, axis=-1) - d_log / (1.0 - raw_keys)
    term_ref[0:1, :] += jnp.sum(e * (1.0 - sig), axis=0, keepdims=True)
    d_query_ref[0, :, share:] = (-e * slack * sig * (1.0 - sig)).astype(jnp.bfloat16)


def row_block(step, order_ref):
    return (order_ref[step], 0, 0)


def state_block(step, order_ref):
    return (order_ref[step], 0, 0, 0)


def fixed_block(step, order_ref):
    return (0, 0)


def run_forward(order, queries, values, slack, gain):
    blocks, span, columns = queries.shape
    share = columns // 2
    heads = share // HEAD
    return pl.pallas_call(
        forward_kernel,
        grid_spec=pltpu.PrefetchScalarGridSpec(
            num_scalar_prefetch=1,
            grid=(blocks,),
            in_specs=[
                pl.BlockSpec((1, span, columns), row_block),
                pl.BlockSpec((1, span, columns), row_block),
                pl.BlockSpec((1, share), fixed_block),
                pl.BlockSpec((1, share), fixed_block),
            ],
            out_specs=[
                pl.BlockSpec((1, span, share), row_block),
                pl.BlockSpec((1, span, share), row_block),
                pl.BlockSpec((1, heads, HEAD, HEAD), state_block),
            ],
            scratch_shapes=[pltpu.VMEM((heads, HEAD, HEAD), jnp.float32)],
        ),
        out_shape=[
            jax.ShapeDtypeStruct((blocks, span, share), jnp.bfloat16),
            jax.ShapeDtypeStruct((blocks, span, share), jnp.float32),
            jax.ShapeDtypeStruct((blocks, heads, HEAD, HEAD), jnp.float32),
        ],
        compiler_params=pltpu.CompilerParams(vmem_limit_bytes=VMEM_BYTES),
        cost_estimate=pl.CostEstimate(
            flops=150 * queries.size * span, bytes_accessed=20 * queries.size, transcendentals=0
        ),
        name="recurrence_forward",
    )(order, queries, values, slack, gain)


def run_backward(order, queries, values, slack, gain, mixed, states, d_unit):
    blocks, span, columns = queries.shape
    share = columns // 2
    heads = share // HEAD
    return pl.pallas_call(
        backward_kernel,
        grid_spec=pltpu.PrefetchScalarGridSpec(
            num_scalar_prefetch=1,
            grid=(blocks,),
            in_specs=[
                pl.BlockSpec((1, span, columns), row_block),
                pl.BlockSpec((1, span, columns), row_block),
                pl.BlockSpec((1, share), fixed_block),
                pl.BlockSpec((1, share), fixed_block),
                pl.BlockSpec((1, span, share), row_block),
                pl.BlockSpec((1, heads, HEAD, HEAD), state_block),
                pl.BlockSpec((1, span, share), row_block),
            ],
            out_specs=[
                pl.BlockSpec((1, span, columns), row_block),
                pl.BlockSpec((1, span, columns), row_block),
                pl.BlockSpec((2, share), fixed_block),
            ],
            scratch_shapes=[
                pltpu.VMEM((heads, HEAD, HEAD), jnp.float32),
                pltpu.VMEM((1, share), jnp.float32),
            ],
        ),
        out_shape=[
            jax.ShapeDtypeStruct((blocks, span, columns), jnp.bfloat16),
            jax.ShapeDtypeStruct((blocks, span, columns), jnp.bfloat16),
            jax.ShapeDtypeStruct((2, share), jnp.float32),
        ],
        compiler_params=pltpu.CompilerParams(vmem_limit_bytes=VMEM_BYTES),
        cost_estimate=pl.CostEstimate(
            flops=250 * queries.size * span, bytes_accessed=30 * queries.size, transcendentals=0
        ),
        name="recurrence_backward",
    )(order, queries, values, slack, gain, mixed, states, d_unit)


def inverse_rms(values):
    return lax.rsqrt(jnp.mean(values * values, axis=-1, keepdims=True) + 1e-06)


def unscaled_grad(d_scaled, scaled, inverse):
    return inverse * (d_scaled - scaled * jnp.mean(d_scaled * scaled, axis=-1, keepdims=True))


def on_device(
    inputs,
    cotangent,
    norm_gain,
    mixer_gain,
    ffn_gain,
    slack,
    w_query,
    w_forget,
    w_input,
    w_gate_out,
    w_out,
    w_gate,
    w_up,
    w_down,
):
    width = inputs.shape[-1]
    dp, count, here = lax.axis_size("dp"), ranks(), rank()
    float32, bfloat16 = jnp.float32, jnp.bfloat16
    sending, taking = turns(1), turns(-1)
    mixer_weights = (w_query, w_forget, w_input, w_gate_out)
    ffn_weights = (w_gate, w_up)
    core, big = 1, dp // 2
    in_place = 2 * w_out.shape[0] == HEAD
    chunks = dp if in_place else 1

    def to_rank(rows):
        return rows if in_place else to_users(rows)

    def from_rank(rows):
        return rows if in_place else to_owners(rows)

    gains = jnp.stack([norm_gain, ffn_gain, mixer_gain, slack], axis=1)
    gains = jnp.pad(gains, ((0, 0), (0, LANES - gains.shape[1])))
    cut = traded(cut_columns(sending, (w_query, w_forget, gains, w_input, w_gate_out), chunks))
    own_in, own_d = to_side(inputs, cotangent)
    mixer_out = peers_gather(to_rank(w_out))
    own_in, own_d, cut = sync(own_in, own_d, cut)

    by_big, by_side = ((big, 0), functools.partial(across, bit=big)), ((0, 1), swapped)
    first_in = gather_first(own_in)
    split = 2 * (width // count) + LANES
    query_cut, value_cut = halves(cut, split)
    query_near = jnp.stack([query_cut, across(query_cut, big)])
    value_near = jnp.stack([value_cut, swapped(value_cut)])
    cut = cut_columns(sending, (w_gate, w_up), chunks)
    first_in, query_near, value_near, own_d, cut, mixer_out = sync(
        first_in, query_near, value_near, own_d, cut, mixer_out
    )

    second_in = gather_second(first_in)
    query_far = swapped(query_near)
    value_far = across(value_near, big)
    waiting = list(cut[1:])
    cut = [cut[0], turned(waiting[0], 1)]
    second_in, query_far, value_far, cut, waiting, own_d = sync(
        second_in, query_far, value_far, cut, waiting, own_d
    )

    query_blocks = (query_near, query_far, across(query_near, core), across(query_far, core))
    value_blocks = (value_near, value_far, across(value_near, core), across(value_far, core))
    raw_in = gathered(own_in, first_in, second_in)
    raw_in, query_blocks, value_blocks, cut, waiting, own_d, late_down = sync(
        raw_in, query_blocks, value_blocks, cut, waiting, own_d, w_down
    )

    down = peers_gather(to_rank(late_down))
    for turn in range(2, count):
        cut = cut + [turned(waiting[turn - 1], turn)]
    share = 2 * (width // count)
    query_in, gains = assembled(*query_blocks, False, (share, LANES))
    (value_in,) = assembled(*value_blocks, True, (share,))
    gains = jnp.transpose(gains)[:4].astype(float32)
    gain_first, gain_second = gains[0], gains[1]
    here_gains = pick(gains.reshape(4, chunks, count, -1), here, 2).reshape(4, -1)[2:]
    mixer_gain_here, slack_here = here_gains[:1], here_gains[1:]
    all_tokens = raw_in.astype(float32)
    rows_in = (all_tokens * inverse_rms(all_tokens) * gain_first).astype(bfloat16)
    queries = matmul(rows_in, query_in).reshape(count, -1, share)
    values = matmul(rows_in, value_in).reshape(count, -1, share)
    queries, values, cut = sync(queries, values, cut)

    units = cut[0].shape[-1] // 2
    gate_cut, up_cut = halves(cut, units)
    gate_near, up_near = across(gate_cut, big), swapped(up_cut)
    unit, mixed, states = run_forward(taking, queries, values, slack_here, mixer_gain_here)
    unit, mixed, states, gate_near, up_near = sync(unit, mixed, states, gate_near, up_near)
    gate_near, up_near = jnp.stack([gate_cut, gate_near]), jnp.stack([up_cut, up_near])
    rows_unit = unit.reshape(-1, unit.shape[-1])
    branch_terms = by_turn(matmul(away_rows(rows_unit), mixer_out))
    branch_terms, gate_near, up_near, own_d = sync(branch_terms, gate_near, up_near, own_d)

    branch_first = scatter_first(branch_terms)
    branch_own = matmul(own_rows(rows_unit), mixer_out)
    gate_far = swapped(gate_near)
    up_far = across(up_near, big)
    rows_d = lax.all_gather(own_d, "fsdp", axis_index_groups=rank_groups())
    branch_first, branch_own, gate_near, up_near, gate_far, up_far, branch_terms = sync(
        branch_first, branch_own, gate_near, up_near, gate_far, up_far, branch_terms
    )

    branch_second = scatter_second(branch_terms, branch_first)
    gate_blocks = (gate_near, gate_far, across(gate_near, core))
    up_blocks = (up_near, up_far, across(up_near, core))
    tokens = own_in.astype(float32)
    hidden = tokens + scattered(branch_own, branch_first, branch_second)
    second_inverse = inverse_rms(hidden)
    hidden_hat = hidden * second_inverse
    own_mid = (hidden_hat * gain_second).astype(bfloat16)
    own_mid, gate_blocks, up_blocks, down = sync(own_mid, gate_blocks, up_blocks, down)

    mid_step = gather_first(own_mid)
    gate_blocks = gate_blocks + (across(gate_blocks[1], core),)
    up_blocks = up_blocks + (across(up_blocks[1], core),)
    (gate_in,) = assembled(*gate_blocks, False, (units,))
    (up_in,) = assembled(*up_blocks, True, (units,))
    mid_step, gate_in = sync(mid_step, gate_in)
    mid_last = gather_second(mid_step)
    mid_last, rows_d, up_in = sync(mid_last, rows_d, up_in)
    rows_mid = gathered(own_mid, mid_step, mid_last)
    gate_proj = matmul(rows_mid, gate_in)
    up_proj = matmul(rows_mid, up_in)
    rows_d = jnp.concatenate(reordered(rows_d), axis=0)
    sig = jax.nn.sigmoid(gate_proj)
    inner = (gate_proj * sig * up_proj).astype(bfloat16)
    d_inner = back_product(rows_d, down)
    d_gate = (d_inner * up_proj * sig * (1.0 + gate_proj * (1.0 - sig))).astype(bfloat16)
    d_up = (d_inner * gate_proj * sig).astype(bfloat16)

    def hidden_product(cut):
        return back_product(cut(d_gate), gate_in) + back_product(cut(d_up), up_in)

    mid_terms = by_turn(hidden_product(away_rows))
    mid_terms, d_gate, d_up, inner = sync(mid_terms, d_gate, d_up, inner)

    mid_first = scatter_first(mid_terms)
    mid_own = hidden_product(own_rows)
    halves_mid = core_halves(rows_mid)
    gate_given, up_given = core_given(halves_mid, d_gate), core_given(halves_mid, d_up)
    mid_first, mid_own, mid_terms, halves_mid, inner, gate_given, up_given = sync(
        mid_first, mid_own, mid_terms, halves_mid, inner, gate_given, up_given
    )

    mid_second = scatter_second(mid_terms, mid_first)
    gate_got, up_got = across(gate_given, core), across(up_given, core)
    marks = block_marks()
    d_hidden = own_d.astype(float32) + unscaled_grad(
        scattered(mid_own, mid_first, mid_second) * gain_second, hidden_hat, second_inverse
    )
    own_branch, gate_got, up_got, inner, halves_mid = sync(
        d_hidden.astype(bfloat16), gate_got, up_got, inner, halves_mid
    )

    all_branch = gather_first(own_branch, False)
    gate_total = core_sum(halves_mid, d_gate, gate_got)
    up_total = core_sum(halves_mid, d_up, up_got)
    gate_total, gate_marks = shrunk((gate_total, marks), by_side)
    up_total, up_marks = shrunk((up_total, marks), by_big)
    out_part = matmul(inner, down).astype(bfloat16).reshape(count, -1, width)
    out_part = jnp.stack(reordered(out_part))
    down_term = outer_sum(inner, rows_d).astype(bfloat16)
    halves_in = core_halves(rows_in)
    all_branch, gate_total, up_total, out_part, halves_in, down_term = sync(
        all_branch, gate_total, up_total, out_part, halves_in, down_term
    )

    out_part = lax.psum_scatter(
        out_part, "fsdp", scatter_dimension=0, axis_index_groups=rank_groups()
    )
    gate_total, _ = shrunk((gate_total, gate_marks), by_big)
    up_total, _ = shrunk((up_total, up_marks), by_side)

    def parts(*totals):
        picked = [[pick(total, sending[turn]) for total in totals] for turn in range(count)]
        return [jnp.concatenate(pieces, axis=-1) for pieces in picked]

    rows_branch = gathered_directly(own_branch, all_branch)
    d_unit = back_product(rows_branch, mixer_out).reshape(count, -1, mixer_out.shape[0])
    d_queries, d_values, terms = run_backward(
        taking[::-1], queries, values, slack_here, mixer_gain_here, mixed, states, d_unit
    )
    d_queries, d_values, terms, gate_total, up_total = sync(
        d_queries, d_values, terms, gate_total, up_total
    )
    d_queries = d_queries.reshape(-1, share)
    d_values = d_values.reshape(-1, share)

    def token_product(cut):
        return back_product(cut(d_queries), query_in) + back_product(cut(d_values), value_in)

    in_terms = by_turn(token_product(away_rows))
    waiting = parts(gate_total, up_total)
    in_terms, d_queries, d_values, terms, waiting, down_term = sync(
        in_terms, d_queries, d_values, terms, waiting, down_term
    )

    in_first = scatter_first(in_terms)
    query_total = core_sum(halves_in, d_queries, across(core_given(halves_in, d_queries), core))
    value_total = core_sum(halves_in, d_values, across(core_given(halves_in, d_values), core))
    in_own = token_product(own_rows)
    terms = terms + across(terms, core)
    in_first, in_own, query_total, value_total, terms, in_terms, rows_branch, waiting, out_part = sync(
        in_first, in_own, query_total, value_total, terms, in_terms, rows_branch, waiting, out_part
    )

    in_second = scatter_second(in_terms, in_first)
    query_next, query_marks = shrunk((query_total, marks), by_side)
    value_next, value_marks = shrunk((value_total, marks), by_big)
    out_term = outer_sum(rows_unit, rows_branch).astype(bfloat16)
    peer_terms = [term.reshape(2 * dp, -1, width) for term in (out_term, down_term)]
    peer_sum = peers_scatter(jnp.concatenate(peer_terms, axis=1).reshape(-1, width))
    ffn_parts = [waiting[0], turned(waiting[1], 1)]
    in_second, query_total, value_total, terms, ffn_parts, waiting = sync(
        in_second, query_next, value_next, terms, ffn_parts, waiting
    )

    ffn_parts = ffn_parts + [turned(waiting[turn], turn) for turn in range(2, count)]

    query_total, _ = shrunk((query_total, query_marks), by_big)
    value_total, _ = shrunk((value_total, value_marks), by_side)
    terms = terms + swapped(terms)
    first_inverse = inverse_rms(tokens)
    d_normed = scattered(in_own, in_first, in_second)
    input_grad = d_hidden + unscaled_grad(
        d_normed * gain_first, tokens * first_inverse, first_inverse
    )
    output = hidden + out_part.astype(float32)
    query_total, value_total, terms, input_grad, output, ffn_parts = sync(
        query_total, value_total, terms, input_grad, output, ffn_parts
    )

    waiting = parts(query_total, value_total)
    mixer_parts = [waiting[0]] + [turned(waiting[turn], turn) for turn in range(1, count)]
    ffn_parts, mixer_first = sync(ffn_parts, mixer_parts[1])
    mixer_parts = mixer_parts[:1] + [mixer_first] + mixer_parts[2:]
    grads_ffn, ffn_product = join_columns(taking, ffn_parts, ffn_weights, chunks)
    out_rows = w_out.shape[0]
    grad_out, grad_down = from_rank(peer_sum[:out_rows]), from_rank(peer_sum[out_rows:])
    output, input_grad = from_side(output, input_grad)
    terms = terms + across(terms, big)
    terms = from_rank(pick(terms.reshape(2, 2 * dp, -1), 2 * lax.axis_index("dp") + side(), 1))
    mixer_parts, ffn_product = sync(mixer_parts, ffn_product)
    grads_mixer, mixer_product = join_columns(taking, mixer_parts, mixer_weights, chunks)

    return (
        output,
        input_grad,
        mixer_product / norm_gain.astype(float32),
        terms[1],
        ffn_product / ffn_gain.astype(float32),
        terms[0],
        *grads_mixer,
        grad_out.astype(float32),
        *grads_ffn,
        grad_down.astype(float32),
    )


def solution(mesh):
    in_specs = (
        P(None, "dp", "fsdp", None),
        P(None, "dp", "fsdp", None),
        P(("dp", "fsdp")),
        P(("dp", "fsdp")),
        P(("dp", "fsdp")),
        P(("dp", "fsdp")),
        P(("dp", "fsdp"), None),
        P(("dp", "fsdp"), None),
        P(("dp", "fsdp"), None),
        P(("dp", "fsdp"), None),
        P(("dp", "fsdp"), None),
        P(("dp", "fsdp"), None),
        P(("dp", "fsdp"), None),
        P(("dp", "fsdp"), None),
    )
    out_specs = (
        P(None, "dp", "fsdp", None),
        P(None, "dp", "fsdp", None),
        P(("dp", "fsdp")),
        P(("dp", "fsdp")),
        P(("dp", "fsdp")),
        P(("dp", "fsdp")),
        P(("dp", "fsdp"), None),
        P(("dp", "fsdp"), None),
        P(("dp", "fsdp"), None),
        P(("dp", "fsdp"), None),
        P(("dp", "fsdp"), None),
        P(("dp", "fsdp"), None),
        P(("dp", "fsdp"), None),
        P(("dp", "fsdp"), None),
    )
    return jax.shard_map(
        on_device, mesh=mesh, in_specs=in_specs, out_specs=out_specs, check_vma=False
    )
```

```python
import functools

import jax
import jax.numpy as jnp
from jax import lax
from jax.experimental import pallas as pl
from jax.experimental.pallas import tpu as pltpu
from jax.sharding import PartitionSpec as P

HEAD = 128
LANES = 128
VMEM_BYTES = 24 * 1024 * 1024
HIGHEST = lax.Precision.HIGHEST
NN = (((1,), (0,)), ((), ()))
NT = (((1,), (1,)), ((), ()))
TN = (((0,), (0,)), ((), ()))


def ranks():
    return lax.axis_size("fsdp") // 2


def rank():
    return lax.axis_index("fsdp") // 2


def side():
    return lax.axis_index("fsdp") % 2


def pick(array, index, axis=0):
    return lax.dynamic_index_in_dim(array, index, axis, False)


def swapped(array):
    count = lax.axis_size("fsdp")
    return lax.ppermute(array, "fsdp", [(i, i ^ 1) for i in range(count)])


def turned(array, turn):
    count = lax.axis_size("fsdp")
    return lax.ppermute(array, "fsdp", [(i, (i + 2 * turn) % count) for i in range(count)])


def across(array, bit):
    count = lax.axis_size("dp")
    return lax.ppermute(array, "dp", [(i, i ^ bit) for i in range(count)])


def placed(pieces):
    whole = jnp.zeros((len(pieces),) + pieces[0][1].shape, pieces[0][1].dtype)
    for index, piece in pieces:
        whole = lax.dynamic_update_index_in_dim(whole, piece, index, 0)
    return whole


def to_side(*arrays):
    here = side()
    got = swapped(jnp.concatenate([pick(array, 1 - here) for array in arrays], axis=0))
    both = [placed([(here, pick(a, here)[0]), (1 - here, piece)]) for a, piece in zip(arrays, got)]
    return [rows.reshape((-1,) + rows.shape[2:]) for rows in both]


def from_side(*arrays):
    here = side()
    halves = [rows.reshape((2, 1, rows.shape[0] // 2) + rows.shape[1:]) for rows in arrays]
    got = swapped(jnp.concatenate([pick(half, 1 - here) for half in halves], axis=0))
    return [
        placed([(here, pick(half, here)), (1 - here, piece[None])]) for half, piece in zip(halves, got)
    ]


def shifted(array, step, among=None):
    count = ranks()
    starts = [r for r in (range(count) if among is None else among) if 0 <= r + step < count]
    moves = [(2 * r + s, 2 * (r + step) + s) for r in starts for s in range(2)]
    return lax.ppermute(array, "fsdp", moves)


def ends_traded(array):
    last = lax.axis_size("fsdp") - 2
    moves = [(s, last + s) for s in range(2)] + [(last + s, s) for s in range(2)]
    return lax.ppermute(array, "fsdp", moves)


def gather_first(own, relay=True):
    if ranks() != 4 or not relay:
        return [turned(own, turn) for turn in range(1, ranks())]
    return [shifted(own, 1), shifted(own, -1), ends_traded(own)]


def gather_second(first):
    return [] if ranks() != 4 else [shifted(first[0], 1, (1, 2)), shifted(first[1], -1, (1, 2))]


def gathered_directly(own, pieces):
    return jnp.concatenate([own] + pieces, axis=0)


def gathered(own, first, second):
    here = rank()
    if ranks() != 4:
        return jnp.concatenate([own] + first, axis=0)
    up, down, ends = first
    up2, down2 = second
    near = [jnp.where(here == 0, ends, up), jnp.where(here >= 2, up2, down2)]
    return jnp.concatenate([own] + near + [jnp.where(here == 3, ends, down)], axis=0)


def away_rows(operand):
    return operand[operand.shape[0] // ranks() :]


def own_rows(operand):
    return operand[: operand.shape[0] // ranks()]


def by_turn(away):
    return jnp.split(away.astype(jnp.bfloat16), ranks() - 1, axis=0)


def scatter_first(terms):
    if ranks() != 4:
        return [turned(term, -turn - 1) for turn, term in enumerate(terms)]
    ends = jnp.where(rank() == 0, terms[0], terms[2])
    return [shifted(terms[1], 1, (0, 1)), shifted(terms[1], -1, (2, 3)), ends_traded(ends)]


def scatter_second(terms, first):
    if ranks() != 4:
        return []
    up = terms[2].astype(jnp.float32) + first[0].astype(jnp.float32)
    down = terms[0].astype(jnp.float32) + first[1].astype(jnp.float32)
    return [shifted(up.astype(jnp.bfloat16), 1), shifted(down.astype(jnp.bfloat16), -1)]


def scattered(own, first, second):
    for piece in first if ranks() != 4 else first[2:] + second:
        own = own + piece.astype(jnp.float32)
    return own


def sync(*arrays):
    return lax.optimization_barrier(arrays)


def dp_bits():
    bits, bit = [], 1
    while bit < lax.axis_size("dp"):
        bits.append(bit)
        bit *= 2
    return bits


def routes(side_first):
    bits = [((bit, 0), functools.partial(across, bit=bit)) for bit in reversed(dp_bits())]
    return [((0, 1), swapped)] + bits if side_first else bits[:-1] + [((0, 1), swapped)] + bits[-1:]


def user_moves():
    dp, fsdp = lax.axis_size("dp"), lax.axis_size("fsdp")
    moves = []
    for block in range(dp * fsdp):
        user, part = divmod(block, 2 * dp)
        moves.append((block, (part // 2) * fsdp + 2 * user + part % 2))
    return moves


def to_users(rows):
    return lax.ppermute(rows, ("dp", "fsdp"), user_moves())


def to_owners(rows):
    return lax.ppermute(rows, ("dp", "fsdp"), [(b, a) for a, b in user_moves()])


def for_rank(wanted, body, aligned):
    if aligned:
        body(wanted)
        return
    for number in range(ranks()):
        pl.when(wanted == number)(functools.partial(body, number))


def columns_of(number, chunk, weight, chunks, count):
    width = weight.shape[1] // (chunks * count)
    start = chunk * (weight.shape[1] // chunks) + number * width
    return pl.ds(start if isinstance(number, int) else pl.multiple_of(start, LANES), width)


def cut_kernel(order_ref, *refs, chunks):
    count = order_ref.shape[0]
    weights, pieces = refs[:-count], refs[-count:]
    for turn in range(count):

        def cut(number, turn=turn):
            start = 0
            for weight in weights:
                if weight.shape[1] == LANES:
                    pieces[turn][:, start : start + LANES] = weight[...]
                    start += LANES
                    continue
                for chunk in range(chunks):
                    columns = columns_of(number, chunk, weight, chunks, count)
                    pieces[turn][:, start : start + columns.size] = weight[:, columns]
                    start += columns.size

        widths = [w.shape[1] // (chunks * count) for w in weights if w.shape[1] != LANES]
        for_rank(order_ref[turn], cut, all(width % LANES == 0 for width in widths))


def cut_columns(order, weights, chunks):
    count = ranks()
    rows = weights[0].shape[0]
    vmem = pl.BlockSpec(memory_space=pltpu.VMEM)
    width = sum(LANES if w.shape[1] == LANES else w.shape[1] // count for w in weights)
    return pl.pallas_call(
        functools.partial(cut_kernel, chunks=chunks),
        in_specs=[pl.BlockSpec(memory_space=pltpu.SMEM)] + [vmem] * len(weights),
        out_specs=[vmem] * count,
        out_shape=[jax.ShapeDtypeStruct((rows, width), weights[0].dtype)] * count,
        compiler_params=pltpu.CompilerParams(vmem_limit_bytes=VMEM_BYTES),
        name="cut_columns",
    )(order, *weights)


def join_kernel(order_ref, *refs, chunks):
    count = order_ref.shape[0]
    parts = (len(refs) - count - 1) // 2
    pieces, weights = refs[:count], refs[count : count + parts]
    grads, product = refs[count + parts : -1], refs[-1]
    product[...] = jnp.zeros(product.shape, jnp.float32)
    for turn in range(count):

        def join(number, turn=turn):
            start = 0
            total = jnp.zeros(product.shape, jnp.float32)
            for weight, grad in zip(weights, grads):
                for chunk in range(chunks):
                    columns = columns_of(number, chunk, weight, chunks, count)
                    piece = pieces[turn][:, start : start + columns.size].astype(jnp.float32)
                    grad[:, columns] = piece
                    term = piece * weight[:, columns].astype(jnp.float32)
                    total = total + jnp.sum(term, axis=1, keepdims=True)
                    start += columns.size
            product[...] += total

        widths = [w.shape[1] // (chunks * count) for w in weights]
        for_rank(order_ref[turn], join, all(width % LANES == 0 for width in widths))


def join_columns(order, pieces, weights, chunks):
    rows = weights[0].shape[0]
    vmem = pl.BlockSpec(memory_space=pltpu.VMEM)
    *grads, product = pl.pallas_call(
        functools.partial(join_kernel, chunks=chunks),
        in_specs=[pl.BlockSpec(memory_space=pltpu.SMEM)] + [vmem] * (len(pieces) + len(weights)),
        out_specs=[vmem] * (len(weights) + 1),
        out_shape=[jax.ShapeDtypeStruct(w.shape, jnp.float32) for w in weights]
        + [jax.ShapeDtypeStruct((rows, 1), jnp.float32)],
        compiler_params=pltpu.CompilerParams(vmem_limit_bytes=VMEM_BYTES),
        cost_estimate=pl.CostEstimate(
            flops=0, bytes_accessed=40 * sum(w.size for w in weights), transcendentals=0
        ),
        name="join_columns",
    )(order, *pieces, *weights)
    return grads, product[:, 0]


def assemble_kernel(place_ref, *refs, marks):
    (*blocks, sems), wholes = refs[:4] + refs[-1:], refs[4:-1]
    count = blocks[0].shape[1]
    dp_index, here, first_rank = place_ref[0], place_ref[1], place_ref[2]
    copies = []
    for core in range(2):
        for outer in range(2):
            block = blocks[2 * core + outer]
            for inner in range(2):
                dp_mark, side_mark = marks[outer][inner]
                spot = jnp.bitwise_xor(dp_index, dp_mark + core)
                its_side = jnp.bitwise_xor(here, side_mark)
                for turn in range(count):
                    its_rank = lax.rem(first_rank - turn + count, count)
                    start = 0
                    for whole in wholes:
                        columns = whole.shape[-1]
                        source = block.at[inner, turn, :, pl.ds(start, columns)]
                        target = whole.at[spot, its_rank, its_side]
                        copies.append(pltpu.make_async_copy(source, target, sems.at[len(copies)]))
                        copies[-1].start()
                        start += columns
    for copy in copies:
        copy.wait()


def assembled(near, far, near_core, far_core, side_first, widths):
    dp, (_, count, rows, _) = lax.axis_size("dp"), near.shape
    big = dp // 2
    marks = (((0, 0), (0, 1)), ((big, 0), (big, 1))) if side_first else (((0, 0), (big, 0)), ((0, 1), (big, 1)))
    place = jnp.stack([lax.axis_index("dp"), side(), rank()]).astype(jnp.int32)
    anywhere = pl.BlockSpec(memory_space=pl.ANY)
    wholes = pl.pallas_call(
        functools.partial(assemble_kernel, marks=marks),
        in_specs=[pl.BlockSpec(memory_space=pltpu.SMEM)] + [anywhere] * 4,
        out_specs=[pl.BlockSpec(memory_space=pltpu.VMEM)] * len(widths),
        out_shape=[
            jax.ShapeDtypeStruct((dp, count, 2, rows, columns), near.dtype) for columns in widths
        ],
        scratch_shapes=[pltpu.SemaphoreType.DMA((8 * count * len(widths),))],
        compiler_params=pltpu.CompilerParams(vmem_limit_bytes=VMEM_BYTES),
        cost_estimate=pl.CostEstimate(flops=0, bytes_accessed=64 * near.size, transcendentals=0),
        name="assemble_rows",
    )(place, near, far, near_core, far_core)
    return [whole.reshape(-1, whole.shape[-1]) for whole in wholes]


def halves_kernel(*refs):
    *pieces, first, second = refs
    split = first.shape[2]
    for turn, piece in enumerate(pieces):
        first[turn] = piece[:, :split]
        second[turn] = piece[:, split:]


def halves(pieces, split):
    count, (rows, width) = len(pieces), pieces[0].shape
    vmem = pl.BlockSpec(memory_space=pltpu.VMEM)
    return pl.pallas_call(
        halves_kernel,
        in_specs=[vmem] * count,
        out_specs=[vmem] * 2,
        out_shape=[
            jax.ShapeDtypeStruct((count, rows, columns), pieces[0].dtype)
            for columns in (split, width - split)
        ],
        compiler_params=pltpu.CompilerParams(vmem_limit_bytes=VMEM_BYTES),
        name="stack_halves",
    )(*pieces)


def traded(pieces):
    return [pieces[0]] + [turned(piece, turn) for turn, piece in enumerate(pieces) if turn]


def turns(step):
    return (rank() + step * jnp.arange(ranks(), dtype=jnp.int32) + ranks()) % ranks()


def split_kernel(core_ref, rows_ref, own_ref, other_ref, *, block):
    for number in range(own_ref.shape[1] // block):
        there = slice(number * block, (number + 1) * block)
        for index, half_ref in ((core_ref[0], own_ref), (1 - core_ref[0], other_ref)):
            column = pl.multiple_of((2 * number + index) * block, block)
            half_ref[:, there] = rows_ref[:, pl.ds(column, block)]


def core_halves(rows):
    dp, (tokens, width) = lax.axis_size("dp"), rows.shape
    own = (lax.axis_index("dp") % 2).astype(jnp.int32).reshape(1)
    vmem = pl.BlockSpec(memory_space=pltpu.VMEM)
    return pl.pallas_call(
        functools.partial(split_kernel, block=width // dp),
        in_specs=[pl.BlockSpec(memory_space=pltpu.SMEM), vmem],
        out_specs=[vmem] * 2,
        out_shape=[jax.ShapeDtypeStruct((tokens, width // 2), rows.dtype)] * 2,
        compiler_params=pltpu.CompilerParams(vmem_limit_bytes=VMEM_BYTES),
        name="core_halves",
    )(own, rows)


def core_given(rows, grads):
    return outer_sum(rows[1], grads).astype(jnp.bfloat16)


def core_sum(rows, grads, got):
    dp, count = lax.axis_size("dp"), ranks()
    total = (outer_sum(rows[0], grads) + got.astype(jnp.float32)).astype(jnp.bfloat16)
    shape = (2,) * (len(dp_bits()) - 1) + (count, 2, total.shape[0] // (dp * count), total.shape[1])
    return total.reshape(shape)


def shrunk(state, route):
    terms, marks = state
    mark, exchange = route
    axis = marks.index(mark)
    own = (lax.axis_index("dp") // mark[0]) % 2 if mark[0] else side()
    got = exchange(pick(terms, 1 - own, axis))
    total = pick(terms, own, axis).astype(jnp.float32) + got.astype(jnp.float32)
    return (total.astype(jnp.bfloat16), marks[:axis] + marks[axis + 1 :])


def block_marks():
    return [(bit, 0) for bit in reversed(dp_bits()[1:])] + [None, (0, 1)]


def rank_groups():
    count = lax.axis_size("fsdp")
    return [list(range(here, count, 2)) for here in range(2)]


def reordered(blocks):
    return [pick(blocks, (rank() - number + ranks()) % ranks()) for number in range(ranks())]


def peers():
    dp, fsdp = lax.axis_size("dp"), lax.axis_size("fsdp")
    return [[d * fsdp + 2 * r + s for d in range(dp) for s in range(2)] for r in range(fsdp // 2)]


def peers_gather(rows):
    return lax.all_gather(rows, ("dp", "fsdp"), tiled=True, axis_index_groups=peers())


def peers_scatter(terms):
    return lax.psum_scatter(
        terms, ("dp", "fsdp"), scatter_dimension=0, tiled=True, axis_index_groups=peers()
    )


def matmul(left_side, right_side):
    return jnp.dot(left_side, right_side, preferred_element_type=jnp.float32)


def outer_sum(left_side, right_side):
    return lax.dot_general(left_side, right_side, TN, preferred_element_type=jnp.float32)


def back_product(left_side, right_side):
    return lax.dot_general(left_side, right_side, NT, preferred_element_type=jnp.float32)


def dot(left, right, dims, precision=HIGHEST):
    return lax.dot_general(
        left, right, dims, precision=precision, preferred_element_type=jnp.float32
    )


def decayed(forget_proj, slack, lower):
    sig = jax.nn.sigmoid(forget_proj)
    keys = slack * (1.0 - sig)
    running = dot(lower, jnp.log1p(-keys), NN)
    return (sig, keys, running)


def triangle(size):
    rows = lax.broadcasted_iota(jnp.int32, (size, size), 0)
    columns = lax.broadcasted_iota(jnp.int32, (size, size), 1)
    return jnp.where(rows >= columns, 1.0, 0.0)


def normed_head(mixed, gate):
    sig = jax.nn.sigmoid(gate)
    silu = gate * sig
    gated = mixed * silu
    centred = gated - jnp.mean(gated, axis=-1, keepdims=True)
    inv = lax.rsqrt(jnp.mean(centred * centred, axis=-1, keepdims=True) + 1e-05)
    return (sig, silu, inv, centred * inv)


def forward_kernel(
    order_ref, query_ref, value_ref, slack_ref, gain_ref, unit_ref, mixed_ref, states_ref, state
):
    span = query_ref.shape[1]
    share = slack_ref.shape[1]

    @pl.when(pl.program_id(0) == 0)
    def _():
        state[...] = jnp.zeros_like(state)

    states_ref[0] = state[...]
    lower = triangle(span)
    _, keys, running = decayed(query_ref[0, :, share:], slack_ref[...], lower)
    grown = jnp.exp(running)
    queries = query_ref[0, :, :share] * grown
    keys = keys * jnp.exp(-running)
    for head in range(share // HEAD):
        here = slice(head * HEAD, (head + 1) * HEAD)
        gate_here = slice(share + head * HEAD, share + (head + 1) * HEAD)
        values = value_ref[0, :, here]
        before = state[head]
        scores = dot(queries[:, here], keys[:, here], NT) * lower
        mixed = dot(scores, values, NN) + dot(queries[:, here], before, NT)
        state[head] = (before + dot(values, keys[:, here], TN)) * grown[span - 1 :, here]
        mixed_ref[0, :, here] = mixed
        normed = normed_head(mixed, value_ref[0, :, gate_here])[3]
        unit_ref[0, :, here] = (normed * gain_ref[:, here]).astype(jnp.bfloat16)


def backward_kernel(
    order_ref,
    query_ref,
    value_ref,
    slack_ref,
    gain_ref,
    mixed_ref,
    states_ref,
    d_unit_ref,
    d_query_ref,
    d_value_ref,
    term_ref,
    back,
    carry,
):
    span = query_ref.shape[1]
    share = slack_ref.shape[1]

    @pl.when(pl.program_id(0) == 0)
    def _():
        back[...] = jnp.zeros_like(back)
        carry[...] = jnp.zeros_like(carry)
        term_ref[...] = jnp.zeros_like(term_ref)

    lower = triangle(span)
    slack = slack_ref[...]
    sig, raw_keys, running = decayed(query_ref[0, :, share:], slack, lower)
    grown, shrunk = jnp.exp(running), jnp.exp(-running)
    all_queries = query_ref[0, :, :share] * grown
    all_keys = raw_keys * shrunk
    d_running, d_raw_keys = [], []
    for head in range(share // HEAD):
        here = slice(head * HEAD, (head + 1) * HEAD)
        there = slice(share + head * HEAD, share + (head + 1) * HEAD)
        queries, keys = all_queries[:, here], all_keys[:, here]
        values, gate = value_ref[0, :, here], value_ref[0, :, there]
        mixed = mixed_ref[0, :, here]
        d_unit = d_unit_ref[0, :, here]
        sig_gate, silu, inv, normed = normed_head(mixed, gate)
        term_ref[1:2, here] += jnp.sum(d_unit * normed, axis=0, keepdims=True)
        d_n = d_unit * gain_ref[:, here]
        d_gated = inv * (
            d_n
            - jnp.mean(d_n, axis=-1, keepdims=True)
            - normed * jnp.mean(d_n * normed, axis=-1, keepdims=True)
        )
        d_mixed = d_gated * silu
        d_gate = d_gated * mixed * sig_gate * (1.0 + gate * (1.0 - sig_gate))
        d_value_ref[0, :, there] = d_gate.astype(jnp.bfloat16)
        before = states_ref[0, head]
        after_grad = back[head] * grown[span - 1 :, here]
        scores = dot(queries, keys, NT) * lower
        d_scores = dot(d_mixed, values, NT) * lower
        d_queries = dot(d_scores, keys, NN) + dot(d_mixed, before, NN)
        d_keys = dot(d_scores, queries, TN) + dot(values, after_grad, NN)
        d_values = dot(scores, d_mixed, TN) + dot(keys, after_grad, NT)
        before_grad = dot(d_mixed, queries, TN) + after_grad
        d_value_ref[0, :, here] = d_values.astype(jnp.bfloat16)
        d_query_ref[0, :, here] = (d_queries * grown[:, here]).astype(jnp.bfloat16)
        back[head] = before_grad
        d_running.append(queries * d_queries - keys * d_keys)
        d_raw_keys.append(d_keys * shrunk[:, here])
    d_log = dot(lower, jnp.concatenate(d_running, axis=-1), TN) + carry[...]
    for head in range(share // HEAD):
        here = slice(head * HEAD, (head + 1) * HEAD)
        carry[:, here] = jnp.sum(states_ref[0, head] * back[head], axis=0, keepdims=True)
    e = jnp.concatenate(d_raw_keys, axis=-1) - d_log / (1.0 - raw_keys)
    term_ref[0:1, :] += jnp.sum(e * (1.0 - sig), axis=0, keepdims=True)
    d_query_ref[0, :, share:] = (-e * slack * sig * (1.0 - sig)).astype(jnp.bfloat16)


def row_block(step, order_ref):
    return (order_ref[step], 0, 0)


def state_block(step, order_ref):
    return (order_ref[step], 0, 0, 0)


def fixed_block(step, order_ref):
    return (0, 0)


def run_forward(order, queries, values, slack, gain):
    blocks, span, columns = queries.shape
    share = columns // 2
    heads = share // HEAD
    return pl.pallas_call(
        forward_kernel,
        grid_spec=pltpu.PrefetchScalarGridSpec(
            num_scalar_prefetch=1,
            grid=(blocks,),
            in_specs=[
                pl.BlockSpec((1, span, columns), row_block),
                pl.BlockSpec((1, span, columns), row_block),
                pl.BlockSpec((1, share), fixed_block),
                pl.BlockSpec((1, share), fixed_block),
            ],
            out_specs=[
                pl.BlockSpec((1, span, share), row_block),
                pl.BlockSpec((1, span, share), row_block),
                pl.BlockSpec((1, heads, HEAD, HEAD), state_block),
            ],
            scratch_shapes=[pltpu.VMEM((heads, HEAD, HEAD), jnp.float32)],
        ),
        out_shape=[
            jax.ShapeDtypeStruct((blocks, span, share), jnp.bfloat16),
            jax.ShapeDtypeStruct((blocks, span, share), jnp.float32),
            jax.ShapeDtypeStruct((blocks, heads, HEAD, HEAD), jnp.float32),
        ],
        compiler_params=pltpu.CompilerParams(vmem_limit_bytes=VMEM_BYTES),
        cost_estimate=pl.CostEstimate(
            flops=150 * queries.size * span, bytes_accessed=20 * queries.size, transcendentals=0
        ),
        name="recurrence_forward",
    )(order, queries, values, slack, gain)


def run_backward(order, queries, values, slack, gain, mixed, states, d_unit):
    blocks, span, columns = queries.shape
    share = columns // 2
    heads = share // HEAD
    return pl.pallas_call(
        backward_kernel,
        grid_spec=pltpu.PrefetchScalarGridSpec(
            num_scalar_prefetch=1,
            grid=(blocks,),
            in_specs=[
                pl.BlockSpec((1, span, columns), row_block),
                pl.BlockSpec((1, span, columns), row_block),
                pl.BlockSpec((1, share), fixed_block),
                pl.BlockSpec((1, share), fixed_block),
                pl.BlockSpec((1, span, share), row_block),
                pl.BlockSpec((1, heads, HEAD, HEAD), state_block),
                pl.BlockSpec((1, span, share), row_block),
            ],
            out_specs=[
                pl.BlockSpec((1, span, columns), row_block),
                pl.BlockSpec((1, span, columns), row_block),
                pl.BlockSpec((2, share), fixed_block),
            ],
            scratch_shapes=[
                pltpu.VMEM((heads, HEAD, HEAD), jnp.float32),
                pltpu.VMEM((1, share), jnp.float32),
            ],
        ),
        out_shape=[
            jax.ShapeDtypeStruct((blocks, span, columns), jnp.bfloat16),
            jax.ShapeDtypeStruct((blocks, span, columns), jnp.bfloat16),
            jax.ShapeDtypeStruct((2, share), jnp.float32),
        ],
        compiler_params=pltpu.CompilerParams(vmem_limit_bytes=VMEM_BYTES),
        cost_estimate=pl.CostEstimate(
            flops=250 * queries.size * span, bytes_accessed=30 * queries.size, transcendentals=0
        ),
        name="recurrence_backward",
    )(order, queries, values, slack, gain, mixed, states, d_unit)


def inverse_rms(values):
    return lax.rsqrt(jnp.mean(values * values, axis=-1, keepdims=True) + 1e-06)


def unscaled_grad(d_scaled, scaled, inverse):
    return inverse * (d_scaled - scaled * jnp.mean(d_scaled * scaled, axis=-1, keepdims=True))


def on_device(
    inputs,
    cotangent,
    norm_gain,
    mixer_gain,
    ffn_gain,
    slack,
    w_query,
    w_forget,
    w_input,
    w_gate_out,
    w_out,
    w_gate,
    w_up,
    w_down,
):
    width = inputs.shape[-1]
    dp, count, here = lax.axis_size("dp"), ranks(), rank()
    float32, bfloat16 = jnp.float32, jnp.bfloat16
    sending, taking = turns(1), turns(-1)
    mixer_weights = (w_query, w_forget, w_input, w_gate_out)
    ffn_weights = (w_gate, w_up)
    core, big = 1, dp // 2
    in_place = 2 * w_out.shape[0] == HEAD
    chunks = dp if in_place else 1

    def to_rank(rows):
        return rows if in_place else to_users(rows)

    def from_rank(rows):
        return rows if in_place else to_owners(rows)

    gains = jnp.stack([norm_gain, ffn_gain, mixer_gain, slack], axis=1)
    gains = jnp.pad(gains, ((0, 0), (0, LANES - gains.shape[1])))
    cut = traded(cut_columns(sending, (w_query, w_forget, gains, w_input, w_gate_out), chunks))
    own_in, own_d = to_side(inputs, cotangent)
    mixer_out = peers_gather(to_rank(w_out))
    own_in, own_d, cut = sync(own_in, own_d, cut)

    by_big, by_side = ((big, 0), functools.partial(across, bit=big)), ((0, 1), swapped)
    first_in = gather_first(own_in)
    split = 2 * (width // count) + LANES
    query_cut, value_cut = halves(cut, split)
    query_near = jnp.stack([query_cut, across(query_cut, big)])
    value_near = jnp.stack([value_cut, swapped(value_cut)])
    cut = cut_columns(sending, (w_gate, w_up), chunks)
    first_in, query_near, value_near, own_d, cut, mixer_out = sync(
        first_in, query_near, value_near, own_d, cut, mixer_out
    )

    second_in = gather_second(first_in)
    query_far = swapped(query_near)
    value_far = across(value_near, big)
    waiting = list(cut[1:])
    cut = [cut[0], turned(waiting[0], 1)]
    second_in, query_far, value_far, cut, waiting, own_d = sync(
        second_in, query_far, value_far, cut, waiting, own_d
    )

    query_blocks = (query_near, query_far, across(query_near, core), across(query_far, core))
    value_blocks = (value_near, value_far, across(value_near, core), across(value_far, core))
    raw_in = gathered(own_in, first_in, second_in)
    raw_in, query_blocks, value_blocks, cut, waiting, own_d, late_down = sync(
        raw_in, query_blocks, value_blocks, cut, waiting, own_d, w_down
    )

    down = peers_gather(to_rank(late_down))
    for turn in range(2, count):
        cut = cut + [turned(waiting[turn - 1], turn)]
    share = 2 * (width // count)
    query_in, gains = assembled(*query_blocks, False, (share, LANES))
    (value_in,) = assembled(*value_blocks, True, (share,))
    gains = jnp.transpose(gains)[:4].astype(float32)
    gain_first, gain_second = gains[0], gains[1]
    here_gains = pick(gains.reshape(4, chunks, count, -1), here, 2).reshape(4, -1)[2:]
    mixer_gain_here, slack_here = here_gains[:1], here_gains[1:]
    all_tokens = raw_in.astype(float32)
    rows_in = (all_tokens * inverse_rms(all_tokens) * gain_first).astype(bfloat16)
    queries = matmul(rows_in, query_in).reshape(count, -1, share)
    values = matmul(rows_in, value_in).reshape(count, -1, share)
    queries, values, cut = sync(queries, values, cut)

    units = cut[0].shape[-1] // 2
    gate_cut, up_cut = halves(cut, units)
    gate_near, up_near = across(gate_cut, big), swapped(up_cut)
    unit, mixed, states = run_forward(taking, queries, values, slack_here, mixer_gain_here)
    unit, mixed, states, gate_near, up_near = sync(unit, mixed, states, gate_near, up_near)
    gate_near, up_near = jnp.stack([gate_cut, gate_near]), jnp.stack([up_cut, up_near])
    rows_unit = unit.reshape(-1, unit.shape[-1])
    branch_terms = by_turn(matmul(away_rows(rows_unit), mixer_out))
    branch_terms, gate_near, up_near, own_d = sync(branch_terms, gate_near, up_near, own_d)

    branch_first = scatter_first(branch_terms)
    branch_own = matmul(own_rows(rows_unit), mixer_out)
    gate_far = swapped(gate_near)
    up_far = across(up_near, big)
    rows_d = lax.all_gather(own_d, "fsdp", axis_index_groups=rank_groups())
    branch_first, branch_own, gate_near, up_near, gate_far, up_far, branch_terms = sync(
        branch_first, branch_own, gate_near, up_near, gate_far, up_far, branch_terms
    )

    branch_second = scatter_second(branch_terms, branch_first)
    gate_blocks = (gate_near, gate_far, across(gate_near, core))
    up_blocks = (up_near, up_far, across(up_near, core))
    tokens = own_in.astype(float32)
    hidden = tokens + scattered(branch_own, branch_first, branch_second)
    second_inverse = inverse_rms(hidden)
    hidden_hat = hidden * second_inverse
    own_mid = (hidden_hat * gain_second).astype(bfloat16)
    own_mid, gate_blocks, up_blocks, down = sync(own_mid, gate_blocks, up_blocks, down)

    mid_step = gather_first(own_mid)
    gate_blocks = gate_blocks + (across(gate_blocks[1], core),)
    up_blocks = up_blocks + (across(up_blocks[1], core),)
    (gate_in,) = assembled(*gate_blocks, False, (units,))
    (up_in,) = assembled(*up_blocks, True, (units,))
    mid_step, gate_in = sync(mid_step, gate_in)
    mid_last = gather_second(mid_step)
    mid_last, rows_d, up_in = sync(mid_last, rows_d, up_in)
    rows_mid = gathered(own_mid, mid_step, mid_last)
    gate_proj = matmul(rows_mid, gate_in)
    up_proj = matmul(rows_mid, up_in)
    rows_d = jnp.concatenate(reordered(rows_d), axis=0)
    sig = jax.nn.sigmoid(gate_proj)
    inner = (gate_proj * sig * up_proj).astype(bfloat16)
    d_inner = back_product(rows_d, down)
    d_gate = (d_inner * up_proj * sig * (1.0 + gate_proj * (1.0 - sig))).astype(bfloat16)
    d_up = (d_inner * gate_proj * sig).astype(bfloat16)

    def hidden_product(cut):
        return back_product(cut(d_gate), gate_in) + back_product(cut(d_up), up_in)

    mid_terms = by_turn(hidden_product(away_rows))
    mid_terms, d_gate, d_up, inner = sync(mid_terms, d_gate, d_up, inner)

    mid_first = scatter_first(mid_terms)
    mid_own = hidden_product(own_rows)
    halves_mid = core_halves(rows_mid)
    gate_given, up_given = core_given(halves_mid, d_gate), core_given(halves_mid, d_up)
    mid_first, mid_own, mid_terms, halves_mid, inner, gate_given, up_given = sync(
        mid_first, mid_own, mid_terms, halves_mid, inner, gate_given, up_given
    )

    mid_second = scatter_second(mid_terms, mid_first)
    gate_got, up_got = across(gate_given, core), across(up_given, core)
    marks = block_marks()
    d_hidden = own_d.astype(float32) + unscaled_grad(
        scattered(mid_own, mid_first, mid_second) * gain_second, hidden_hat, second_inverse
    )
    own_branch, gate_got, up_got, inner, halves_mid = sync(
        d_hidden.astype(bfloat16), gate_got, up_got, inner, halves_mid
    )

    all_branch = gather_first(own_branch, False)
    gate_total = core_sum(halves_mid, d_gate, gate_got)
    up_total = core_sum(halves_mid, d_up, up_got)
    gate_total, gate_marks = shrunk((gate_total, marks), by_side)
    up_total, up_marks = shrunk((up_total, marks), by_big)
    out_part = matmul(inner, down).astype(bfloat16).reshape(count, -1, width)
    out_part = jnp.stack(reordered(out_part))
    down_term = outer_sum(inner, rows_d).astype(bfloat16)
    halves_in = core_halves(rows_in)
    all_branch, gate_total, up_total, out_part, halves_in, down_term = sync(
        all_branch, gate_total, up_total, out_part, halves_in, down_term
    )

    out_part = lax.psum_scatter(
        out_part, "fsdp", scatter_dimension=0, axis_index_groups=rank_groups()
    )
    gate_total, _ = shrunk((gate_total, gate_marks), by_big)
    up_total, _ = shrunk((up_total, up_marks), by_side)

    def parts(*totals):
        picked = [[pick(total, sending[turn]) for total in totals] for turn in range(count)]
        return [jnp.concatenate(pieces, axis=-1) for pieces in picked]

    rows_branch = gathered_directly(own_branch, all_branch)
    d_unit = back_product(rows_branch, mixer_out).reshape(count, -1, mixer_out.shape[0])
    d_queries, d_values, terms = run_backward(
        taking[::-1], queries, values, slack_here, mixer_gain_here, mixed, states, d_unit
    )
    d_queries, d_values, terms, gate_total, up_total = sync(
        d_queries, d_values, terms, gate_total, up_total
    )
    d_queries = d_queries.reshape(-1, share)
    d_values = d_values.reshape(-1, share)

    def token_product(cut):
        return back_product(cut(d_queries), query_in) + back_product(cut(d_values), value_in)

    in_terms = by_turn(token_product(away_rows))
    waiting = parts(gate_total, up_total)
    in_terms, d_queries, d_values, terms, waiting, down_term = sync(
        in_terms, d_queries, d_values, terms, waiting, down_term
    )

    in_first = scatter_first(in_terms)
    query_total = core_sum(halves_in, d_queries, across(core_given(halves_in, d_queries), core))
    value_total = core_sum(halves_in, d_values, across(core_given(halves_in, d_values), core))
    in_own = token_product(own_rows)
    terms = terms + across(terms, core)
    in_first, in_own, query_total, value_total, terms, in_terms, rows_branch, waiting, out_part = sync(
        in_first, in_own, query_total, value_total, terms, in_terms, rows_branch, waiting, out_part
    )

    in_second = scatter_second(in_terms, in_first)
    query_next, query_marks = shrunk((query_total, marks), by_side)
    value_next, value_marks = shrunk((value_total, marks), by_big)
    out_term = outer_sum(rows_unit, rows_branch).astype(bfloat16)
    peer_terms = [term.reshape(2 * dp, -1, width) for term in (out_term, down_term)]
    peer_sum = peers_scatter(jnp.concatenate(peer_terms, axis=1).reshape(-1, width))
    ffn_parts = [waiting[0], turned(waiting[1], 1)]
    in_second, query_total, value_total, terms, ffn_parts, waiting = sync(
        in_second, query_next, value_next, terms, ffn_parts, waiting
    )

    ffn_parts = ffn_parts + [turned(waiting[turn], turn) for turn in range(2, count)]

    query_total, _ = shrunk((query_total, query_marks), by_big)
    value_total, _ = shrunk((value_total, value_marks), by_side)
    terms = terms + swapped(terms)
    first_inverse = inverse_rms(tokens)
    d_normed = scattered(in_own, in_first, in_second)
    input_grad = d_hidden + unscaled_grad(
        d_normed * gain_first, tokens * first_inverse, first_inverse
    )
    output = hidden + out_part.astype(float32)
    query_total, value_total, terms, input_grad, output, ffn_parts = sync(
        query_total, value_total, terms, input_grad, output, ffn_parts
    )

    waiting = parts(query_total, value_total)
    mixer_parts = [waiting[0]] + [turned(waiting[turn], turn) for turn in range(1, count)]
    ffn_parts, mixer_first = sync(ffn_parts, mixer_parts[1])
    mixer_parts = mixer_parts[:1] + [mixer_first] + mixer_parts[2:]
    grads_ffn, ffn_product = join_columns(taking, ffn_parts, ffn_weights, chunks)
    out_rows = w_out.shape[0]
    grad_out, grad_down = from_rank(peer_sum[:out_rows]), from_rank(peer_sum[out_rows:])
    output, input_grad = from_side(output, input_grad)
    terms = terms + across(terms, big)
    terms = from_rank(pick(terms.reshape(2, 2 * dp, -1), 2 * lax.axis_index("dp") + side(), 1))
    mixer_parts, ffn_product = sync(mixer_parts, ffn_product)
    grads_mixer, mixer_product = join_columns(taking, mixer_parts, mixer_weights, chunks)

    return (
        output,
        input_grad,
        mixer_product / norm_gain.astype(float32),
        terms[1],
        ffn_product / ffn_gain.astype(float32),
        terms[0],
        *grads_mixer,
        grad_out.astype(float32),
        *grads_ffn,
        grad_down.astype(float32),
    )


def solution(mesh):
    in_specs = (
        P(None, "dp", "fsdp", None),
        P(None, "dp", "fsdp", None),
        P(("dp", "fsdp")),
        P(("dp", "fsdp")),
        P(("dp", "fsdp")),
        P(("dp", "fsdp")),
        P(("dp", "fsdp"), None),
        P(("dp", "fsdp"), None),
        P(("dp", "fsdp"), None),
        P(("dp", "fsdp"), None),
        P(("dp", "fsdp"), None),
        P(("dp", "fsdp"), None),
        P(("dp", "fsdp"), None),
        P(("dp", "fsdp"), None),
    )
    out_specs = (
        P(None, "dp", "fsdp", None),
        P(None, "dp", "fsdp", None),
        P(("dp", "fsdp")),
        P(("dp", "fsdp")),
        P(("dp", "fsdp")),
        P(("dp", "fsdp")),
        P(("dp", "fsdp"), None),
        P(("dp", "fsdp"), None),
        P(("dp", "fsdp"), None),
        P(("dp", "fsdp"), None),
        P(("dp", "fsdp"), None),
        P(("dp", "fsdp"), None),
        P(("dp", "fsdp"), None),
        P(("dp", "fsdp"), None),
    )
    return jax.shard_map(
        on_device, mesh=mesh, in_specs=in_specs, out_specs=out_specs, check_vma=False
    )
```
